128 devices in a mesh: src: 8 (over y, core), help: 16 (over z, x).
Axes of the slice: x: 4, y: 4, z: 4, core: 2. Of those that a mesh axis runs over, the one named last changes fastest.
Arguments:
- tiles: int32 [2, 1024], P(None, 'src'), may hold values from 0 to 127, as said below
- cell_slot: int32 [2, 128], replicated, may hold values from 0 to 127, as said below
- counts: int32 [128, 2], P(('src', 'help')), may hold values from 128 to 512, as said below
- src_points: bfloat16 [65536, 512], P(('src', 'help')), may hold values from -9 to 9
- tgt_points: bfloat16 [65536, 512], P(('src', 'help')), may hold values from -9 to 9
Outputs:
- source_potential: float32 [65536], P(('src', 'help'))
- target_potential: float32 [65536], P(('src', 'help'))
- transport: float32 [65536, 512], P(('src', 'help'))
The draws below stay inside these ranges and needn't reach their ends.
Inputs may be any that keep to these rules, and one draw needn't show every extreme that they name: `tiles`: columns come in blocks of 128, block g for group g of 16 cells: a block's source cells have ids g * 16 to g * 16 + 15, its target cells lie in group g or in group g + 1 (group 8 - 1 is followed by group 0); no pair is listed twice, and every source cell and every target cell is named in some column. Each row is a permutation that keeps every cell in its group: cell c is stored at slot cell_slot[side, c], with cell_slot[side, c] // 16 equal to c // 16; slot k is rows k * 512 to k * 512 + 511 of the point arrays. `counts`: rows of a slot at and beyond its count are padding. Both ends of the range occur in each column.
All inputs are finite; a program needn't handle non-finite values.
Results may differ from the reference program's by a relative error of at most 0.004.
Values may be sent and summed in bfloat16 or wider, within the bound.
No kernel may reach another device: no remote copies, remote signals or barrier semaphores. Data moves between devices by JAX's collectives and lax.ppermute only.
A program may use at most 192 MiB of HBM per device.

```python
import math
import jax
import jax.numpy as jnp
from jax import lax

D = 512
P_SIZE = 512
ITERS = 2
GROUP = 16
GROUPS = 8
NCELL = 128
TPG = 128
TILES = 1024


def draw_tiles(key, part):

    def one_group(index):
        group_key = jax.random.fold_in(key, index + 11)
        pair_ids = jnp.arange(2 * GROUP * GROUP, dtype=jnp.int32)
        src_local = pair_ids // (2 * GROUP)
        tgt_local = pair_ids % (2 * GROUP)
        perm_own = jax.random.permutation(jax.random.fold_in(group_key, 4), GROUP)
        perm_next = jax.random.permutation(jax.random.fold_in(group_key, 5), GROUP)
        partner = jnp.where(tgt_local < GROUP, perm_own[tgt_local % GROUP], perm_next[tgt_local % GROUP])
        is_cover = src_local == partner
        ranking = jax.random.permutation(jax.random.fold_in(group_key, 1), GROUP)
        is_hot = ranking[src_local] < min(4, GROUP)
        jitter = jax.random.randint(jax.random.fold_in(group_key, 2), pair_ids.shape, 0, 1024, dtype=jnp.int32)
        scores = jnp.where(is_cover, 1 << 29, is_hot.astype(jnp.int32) * (1 << 21) + jitter * 1024) + pair_ids
        picked = lax.top_k(scores, TPG)[1]
        picked = picked[jax.random.permutation(jax.random.fold_in(group_key, 3), TPG)]
        src_ids = index * GROUP + src_local[picked]
        tgt_group = jnp.where(tgt_local[picked] < GROUP, index, (index + 1) % GROUPS)
        tgt_ids = tgt_group * GROUP + tgt_local[picked] % GROUP
        return jnp.stack([src_ids, tgt_ids])
    blocks = jax.vmap(one_group)(jnp.arange(GROUPS, dtype=jnp.int32))
    return jnp.transpose(blocks, (1, 0, 2)).reshape(2, TILES).astype(jnp.int32)


def draw_cell_slot(key, part):

    def one_block(index):
        shuffled = jax.random.permutation(jax.random.fold_in(key, index + 101), GROUP)
        return index % GROUPS * GROUP + shuffled
    slots = jax.vmap(one_block)(jnp.arange(2 * GROUPS, dtype=jnp.int32))
    return slots.reshape(2, NCELL).astype(jnp.int32)


def draw_counts(key, part):
    counted = jax.random.randint(jax.random.fold_in(key, 7), (NCELL, 2), P_SIZE // 4, P_SIZE + 1, dtype=jnp.int32)
    places = jax.random.randint(jax.random.fold_in(key, 8), (2,), 0, NCELL, dtype=jnp.int32)
    counted = counted.at[places[0], 0].set(P_SIZE).at[(places[0] + 1) % NCELL, 0].set(P_SIZE // 4)
    counted = counted.at[places[1], 1].set(P_SIZE).at[(places[1] + 1) % NCELL, 1].set(P_SIZE // 4)
    return counted


def point_cloud(key, salt, offset_on, cell_spread_on):
    base_key = jax.random.fold_in(key, salt)
    values = jax.random.normal(jax.random.fold_in(base_key, 1), (NCELL * P_SIZE, D), jnp.float32)
    if offset_on:
        strength_table = jnp.array([0.0, 0.0, 0.0, 7.0, 0.0, 9.0, 11.0, 0.0], jnp.float32)
        slot_ids = jnp.arange(NCELL, dtype=jnp.int32) % 8
        strength = strength_table[slot_ids]
        signs = (jax.random.randint(jax.random.fold_in(base_key, 3), (D,), 0, 2, dtype=jnp.int32) * 2 - 1).astype(jnp.float32)
        shift = strength[:, None, None] * signs[None, None, :] * float(D) ** (-0.25)
        values = (values.reshape(NCELL, P_SIZE, D) + shift).reshape(NCELL * P_SIZE, D)
    if cell_spread_on:
        cell_spread = jnp.exp(jax.random.uniform(jax.random.fold_in(base_key, 4), (NCELL, 1, 1), jnp.float32, math.log(0.6), math.log(3.0)))
        values = (values.reshape(NCELL, P_SIZE, D) * cell_spread).reshape(NCELL * P_SIZE, D)
    return jnp.clip(values, -9.0, 9.0).astype(jnp.bfloat16)


def draw_src_points(key, part):
    return point_cloud(key, 501, True, False)


def draw_tgt_points(key, part):
    return point_cloud(key, 502, False, True)


def setup_inputs(seed: int = 0) -> dict:
    seeds = jax.random.split(jax.random.key(seed), 6)
    tiles = draw_tiles(jax.random.fold_in(seeds[5], 71), 0)
    cell_slot = draw_cell_slot(jax.random.fold_in(seeds[5], 71), 0)
    counts = draw_counts(jax.random.fold_in(seeds[5], 71), 0)
    src_points = draw_src_points(jax.random.fold_in(seeds[5], 71), 0)
    tgt_points = draw_tgt_points(jax.random.fold_in(seeds[5], 71), 0)
    return {"tiles": tiles, "cell_slot": cell_slot, "counts": counts, "src_points": src_points, "tgt_points": tgt_points}


EPSILON = 0.2
NEGATIVE = -1e+30

def join_parts(first, second):
    highest = jnp.maximum(first[0], second[0])
    return (highest, first[1] * jnp.exp(first[0] - highest) + second[1] * jnp.exp(second[0] - highest))

def reference(tiles, cell_slot, counts, src_points, tgt_points):
    cost_scale = math.sqrt(D)
    source_cells = src_points.reshape(NCELL, P_SIZE, D)
    target_cells = tgt_points.reshape(NCELL, P_SIZE, D)
    source_half = 0.5 * lax.optimization_barrier(jnp.sum(jnp.square(source_cells.astype(jnp.float32)), axis=2))
    target_half = 0.5 * lax.optimization_barrier(jnp.sum(jnp.square(target_cells.astype(jnp.float32)), axis=2))
    positions = jnp.arange(P_SIZE, dtype=jnp.int32)
    source_live = positions[None, :] < counts[:, 0:1]
    target_live = positions[None, :] < counts[:, 1:2]
    source_slots = jnp.take(cell_slot[0], tiles[0]).astype(jnp.int32)
    target_slots = jnp.take(cell_slot[1], tiles[1]).astype(jnp.int32)
    pairs = (source_slots, target_slots)

    def tile_cost(src_cell, tgt_cell):
        inner = jnp.dot(source_cells[src_cell], target_cells[tgt_cell].T, preferred_element_type=jnp.float32)
        cost_tile = (source_half[src_cell][:, None] + target_half[tgt_cell][None, :] - inner) / cost_scale
        listed = source_live[src_cell][:, None] & target_live[tgt_cell][None, :]
        return (cost_tile, listed)

    def start_tables():
        return (jnp.full((NCELL, P_SIZE), NEGATIVE, jnp.float32), jnp.zeros((NCELL, P_SIZE), jnp.float32))

    def row_pass(target_potential):

        def visit(tables, pair):
            src_cell, tgt_cell = pair
            cost_tile, listed = tile_cost(src_cell, tgt_cell)
            scores = jnp.where(listed, (target_potential[tgt_cell][None, :] - cost_tile) / EPSILON, NEGATIVE)
            part_max = lax.optimization_barrier(jnp.max(scores, axis=1))
            part_sum = lax.optimization_barrier(jnp.sum(jnp.exp(scores - part_max[:, None]), axis=1))
            joined = join_parts((tables[0][src_cell], tables[1][src_cell]), (part_max, part_sum))
            return ((tables[0].at[src_cell].set(joined[0]), tables[1].at[src_cell].set(joined[1])), None)
        tables, unused = lax.scan(visit, start_tables(), pairs)
        return jnp.where(source_live, -EPSILON * (tables[0] + jnp.log(tables[1])), 0.0)

    def col_pass(source_potential):

        def visit(tables, pair):
            src_cell, tgt_cell = pair
            cost_tile, listed = tile_cost(src_cell, tgt_cell)
            scores = jnp.where(listed, (source_potential[src_cell][:, None] - cost_tile) / EPSILON, NEGATIVE)
            part_max = lax.optimization_barrier(jnp.max(scores, axis=0))
            part_sum = lax.optimization_barrier(jnp.sum(jnp.exp(scores - part_max[None, :]), axis=0))
            joined = join_parts((tables[0][tgt_cell], tables[1][tgt_cell]), (part_max, part_sum))
            return ((tables[0].at[tgt_cell].set(joined[0]), tables[1].at[tgt_cell].set(joined[1])), None)
        tables, unused = lax.scan(visit, start_tables(), pairs)
        return jnp.where(target_live, -EPSILON * (tables[0] + jnp.log(tables[1])), 0.0)
    target_potential = jnp.zeros((NCELL, P_SIZE), jnp.float32)
    source_potential = jnp.zeros((NCELL, P_SIZE), jnp.float32)
    for sweep in range(ITERS):
        source_potential = row_pass(target_potential)
        target_potential = col_pass(source_potential)

    def accumulate(sums, pair):
        src_cell, tgt_cell = pair
        cost_tile, listed = tile_cost(src_cell, tgt_cell)
        exponent = (source_potential[src_cell][:, None] + target_potential[tgt_cell][None, :] - cost_tile) / EPSILON
        weight = jnp.where(listed, jnp.exp(exponent), 0.0).astype(jnp.bfloat16)
        numerator = sums[0].at[src_cell].add(jnp.dot(weight, target_cells[tgt_cell], preferred_element_type=jnp.float32))
        denominator = sums[1].at[src_cell].add(lax.optimization_barrier(jnp.sum(weight.astype(jnp.float32), axis=1)))
        return ((numerator, denominator), None)
    start = (jnp.zeros((NCELL, P_SIZE, D), jnp.float32), jnp.zeros((NCELL, P_SIZE), jnp.float32))
    sums, unused = lax.scan(accumulate, start, pairs)
    safe_total = jnp.where(source_live, sums[1], 1.0)
    transport = jnp.where(source_live[:, :, None], sums[0] / safe_total[:, :, None], 0.0)
    return (source_potential.reshape(NCELL * P_SIZE), target_potential.reshape(NCELL * P_SIZE), transport.reshape(NCELL * P_SIZE, D))
```

```python
import functools
import math

import jax
import jax.numpy as jnp
from jax import lax
from jax.experimental import pallas as pl
from jax.experimental.pallas import tpu as pltpu
from jax.sharding import PartitionSpec as P

ITERS = 2
EPSILON = 0.2
LOG2E = 1.0 / math.log(2.0)
DEAD = -1e30
EMPTY = -2e30
MARK = 1024.0
SIDE = 4
PART = 128
WIDTH = 512
SRC_CELLS = 16
TGT_CELLS = 32
TAIL = 16
PAIRS = 128
F32 = jnp.float32
BF16 = jnp.bfloat16
VMEM_LIMIT = 48 * 1024 * 1024


def x_perm(by):
    return [(z * SIDE + x, z * SIDE + (x + by) % SIDE) for z in range(SIDE) for x in range(SIDE)]


def z_perm(by):
    return [(z * SIDE + x, (z + by) % SIDE * SIDE + x) for z in range(SIDE) for x in range(SIDE)]


def to_group(array, by):
    count = lax.axis_size("src")
    return lax.ppermute(array, "src", [(i, (i + by) % count) for i in range(count)])


def to_help(array, perm):
    return lax.ppermute(array, "help", perm)


def lookup(cell_ids, slot_table):
    matches = cell_ids[:, None] == jnp.arange(slot_table.shape[0], dtype=jnp.int32)[None, :]
    return jnp.sum(jnp.where(matches, slot_table[None, :], 0), axis=1)


def spread(points, perm, me):
    parts = [lax.dynamic_slice_in_dim(points, me * PART, PART, 0)]
    for by in range(1, SIDE):
        other = (me + by) % SIDE
        parts.append(to_help(lax.dynamic_slice_in_dim(points, other * PART, PART, 0), perm(by)))
    return jnp.concatenate(parts, axis=0)


def collect(block, perm):
    rows = block.shape[0]
    half = rows // 2
    behind = to_help(block, perm(1))
    ahead = to_help(block, perm(SIDE - 1))
    far_low = to_help(behind[:half], perm(1))
    far_high = to_help(ahead[half:], perm(SIDE - 1))
    return [
        (0, rows, block),
        (rows, rows, behind),
        (3 * rows, rows, ahead),
        (2 * rows, half, far_low),
        (2 * rows + half, half, far_high),
    ]


def ring_parts(array, perm):
    return [array] + [to_help(array, perm(by)) for by in range(1, SIDE)]


def join(parts):
    top = functools.reduce(jnp.maximum, parts)
    total = functools.reduce(jnp.add, [jnp.exp2(part - top) for part in parts])
    return top + jnp.log2(total)


def eye():
    return lax.broadcasted_iota(jnp.int32, (PART, PART), 0) == lax.broadcasted_iota(
        jnp.int32, (PART, PART), 1
    )


def to_lanes(column):
    return jnp.sum(jnp.where(eye(), jnp.broadcast_to(column, (PART, PART)), 0.0), axis=0, keepdims=True)


def to_rows(lane_vector):
    return jnp.transpose(jnp.broadcast_to(lane_vector, (PART, PART)))


def part_of(index):
    return pl.ds(pl.multiple_of(index * PART, PART), PART)


def load_blocks(refs, places, order, target, sem):
    copies = []
    for (start, rows), ref in zip(places, refs):
        for cell in range(rows // PART):
            place = start // PART + cell
            side, place = place // SRC_CELLS, place % SRC_CELLS
            goal = part_of(side * SRC_CELLS + order[place])
            copies.append(
                pltpu.make_async_copy(
                    ref.at[pl.ds(cell * PART, PART)], target.at[goal], sem.at[len(copies)]
                )
            )
    for copy in copies:
        copy.start()
    return copies


def row_sums(starts, targets, table_ref, level_ref, sums_ref, fill):
    def cell(s, carry):
        first, last = starts[s], starts[s + 1]

        def highest(n, top):
            scores = (fill(s, n) if fill is not None else table_ref[n]) + level_ref[pl.ds(targets[n], 1), :]
            return jnp.maximum(top, scores)

        top = lax.fori_loop(first, last, highest, jnp.full((PART, PART), EMPTY, F32))
        top = jnp.max(top, axis=1, keepdims=True)

        def add(n, total):
            return total + jnp.exp2(table_ref[n] + level_ref[pl.ds(targets[n], 1), :] - top)

        total = lax.fori_loop(first, last, add, jnp.zeros((PART, PART), F32))
        total = jnp.sum(total, axis=1, keepdims=True)
        sums_ref[pl.ds(s, 1), :] = to_lanes(top + jnp.log2(total))
        return carry

    lax.fori_loop(0, SRC_CELLS, cell, 0)


def first_kernel(places_s, places_t, scale, starts, targets, s_order, t_order, *refs):
    ns, nt = len(places_s), len(places_t)
    s_refs, t_refs = refs[:ns], refs[ns : ns + nt]
    table_ref, sums_ref, level_ref, live_ref = refs[ns + nt : ns + nt + 4]
    xs, ys, s_sem, t_sem = refs[ns + nt + 4 :]
    copies = load_blocks(s_refs, places_s, s_order, xs, s_sem)
    copies += load_blocks(t_refs, places_t, t_order, ys, t_sem)
    for copy in copies:
        copy.wait()

    def target_cell(t, carry):
        points = ys[part_of(t), :].astype(F32)
        half = to_lanes(jnp.sum(points * points, axis=1, keepdims=True)) * (0.5 * scale)
        level_ref[pl.ds(t, 1), :] = jnp.where(half > 1e7, DEAD, -half)
        return carry

    lax.fori_loop(0, TGT_CELLS, target_cell, 0)

    def source_cell(s, carry):
        mark = xs[part_of(s), :PART].astype(F32)
        dead = jnp.where(eye() & (mark > 0.5 * MARK), DEAD, 0.0)
        live_ref[pl.ds(s, 1), :] = jnp.sum(dead, axis=0, keepdims=True)
        return carry

    lax.fori_loop(0, SRC_CELLS, source_cell, 0)

    def fill(s, n):
        inner = lax.dot_general(
            xs[part_of(s), :],
            ys[part_of(targets[n]), :],
            (((1,), (1,)), ((), ())),
            preferred_element_type=F32,
        )
        inner = inner * scale
        table_ref[n] = inner
        return inner

    row_sums(starts, targets, table_ref, level_ref, sums_ref, fill)


def source_levels(parts, live):
    return jnp.where(live < 0.5 * DEAD, DEAD, -join([part[...] for part in parts]))


def column_kernel(starts, targets, r0, r1, r2, r3, live_ref, table_ref, sums_ref, level_ref, tops, totals):
    level_ref[...] = source_levels((r0, r1, r2, r3), live_ref[...])
    tops[...] = jnp.full(tops.shape, EMPTY, F32)
    totals[...] = jnp.ones(totals.shape, F32)

    def cell(s, carry):
        level = to_rows(level_ref[pl.ds(s, 1), :])

        def tile(n, inner_carry):
            t = targets[n]
            scores = (table_ref[n] + level).reshape(PART // 8, 8, PART)
            old = tops[t]
            top = jnp.maximum(old, jnp.max(scores, axis=0))
            tops[t] = top
            totals[t] = totals[t] * jnp.exp2(old - top) + jnp.sum(jnp.exp2(scores - top[None]), axis=0)
            return inner_carry

        return lax.fori_loop(starts[s], starts[s + 1], tile, carry)

    lax.fori_loop(0, SRC_CELLS, cell, 0)
    tops_all = tops[...]
    top = jnp.max(tops_all, axis=1)
    total = jnp.sum(totals[...] * jnp.exp2(tops_all - top[:, None, :]), axis=1)
    sums_ref[...] = top + jnp.log2(total)


def target_levels(joined, before, after, first_level):
    own = -join([joined[:SRC_CELLS], before])
    following = -join([joined[SRC_CELLS:], after])
    levels = jnp.concatenate([own, following], axis=0)
    return jnp.where(first_level < 0.5 * DEAD, DEAD, levels)


def row_kernel(starts, targets, joined, before, after, first_level, table_ref, sums_ref, level_ref):
    level_ref[...] = target_levels(joined[...], before[...], after[...], first_level[...])
    row_sums(starts, targets, table_ref, level_ref, sums_ref, None)


def pieces(value, count):
    found = []
    for _ in range(count):
        piece = value.astype(BF16).astype(F32)
        found.append(piece)
        value = value - piece
    return found


def transport_kernel(places_t, starts, targets, t_order, joined, before, after, first_level, src_level, table_ref, *refs):
    nt = len(places_t)
    t_refs = refs[:nt]
    out_ref, ys, level_ref, total_ref, t_sem = refs[nt:]
    copies = load_blocks(t_refs, places_t, t_order, ys, t_sem)
    level_ref[...] = target_levels(joined[...], before[...], after[...], first_level[...])
    for copy in copies:
        copy.wait()

    def cell(s, carry):
        row_level = src_level[pl.ds(s, 1), :]
        level = to_rows(row_level)
        total_ref[...] = jnp.zeros(total_ref.shape, F32)

        def tile(n, weight_sum):
            t = targets[n]
            weight = jnp.exp2(table_ref[n] + level_ref[pl.ds(t, 1), :] + level).astype(BF16)
            total_ref[...] += jnp.dot(weight, ys[part_of(t), :], preferred_element_type=F32)
            return weight_sum + weight.astype(F32)

        weight_sum = lax.fori_loop(starts[s], starts[s + 1], tile, jnp.zeros((PART, PART), F32))
        weight_sum = to_lanes(jnp.sum(weight_sum, axis=1, keepdims=True))
        out_ref[s, :PART, :] = total_ref[...].astype(BF16)
        col_level = level_ref[pl.ds(s, 1), :]
        parts = pieces(weight_sum, 2) + pieces(row_level, 3) + pieces(col_level, 3)
        rows = lax.broadcasted_iota(jnp.int32, (TAIL, WIDTH), 0)
        tail = jnp.where(
            rows == 0,
            jnp.concatenate(parts[:4], axis=1),
            jnp.where(rows == 1, jnp.concatenate(parts[4:], axis=1), 0.0),
        )
        out_ref[s, PART:, :] = tail.astype(BF16)
        return carry

    lax.fori_loop(0, SRC_CELLS, cell, 0)


def finish_kernel(counts, got, half_src, half_tgt, src_ref, tgt_ref, map_ref):
    def tail(sender):
        return got[sender, PART:, :].astype(F32)

    def segment(rows, index):
        return rows[index // SIDE : index // SIDE + 1, index % SIDE * PART : (index % SIDE + 1) * PART]

    lanes = lax.broadcasted_iota(jnp.int32, (1, PART), 1)
    rows = lax.broadcasted_iota(jnp.int32, (PART, 1), 0)
    src_live, tgt_live = counts[0, 0], counts[0, 1]
    for q in range(SIDE):
        tails = [tail(q * SIDE + x) for x in range(SIDE)]
        weight_sum = sum(segment(one, 0) + segment(one, 1) for one in tails)
        live = rows + q * PART < src_live
        inverse = jnp.where(live, 1.0 / to_rows(weight_sum), 0.0)
        for chunk in range(WIDTH // PART):
            columns = slice(chunk * PART, (chunk + 1) * PART)
            numerator = sum(got[q * SIDE + x, :PART, columns].astype(F32) for x in range(SIDE))
            map_ref[q * PART : (q + 1) * PART, columns] = jnp.where(live, numerator * inverse, 0.0)
        level = segment(tails[0], 2) + segment(tails[0], 3) + segment(tails[0], 4)
        value = (level + half_src[q : q + 1, :]) * (EPSILON / LOG2E)
        src_ref[q : q + 1, :] = jnp.where(lanes + q * PART < src_live, value, 0.0)
        first = tail(q)
        level = segment(first, 5) + segment(first, 6) + segment(first, 7)
        value = (level + half_tgt[q : q + 1, :]) * (EPSILON / LOG2E)
        tgt_ref[q : q + 1, :] = jnp.where(lanes + q * PART < tgt_live, value, 0.0)


VM = pl.BlockSpec(memory_space=pltpu.VMEM)
SM = pl.BlockSpec(memory_space=pltpu.SMEM)
ANY = pl.BlockSpec(memory_space=pl.ANY)


def call(kernel, out_shape, in_specs, scratch, *args):
    outs = jax.tree.map(lambda _: VM, out_shape)
    return pl.pallas_call(
        kernel,
        out_shape=out_shape,
        in_specs=in_specs,
        out_specs=outs,
        scratch_shapes=scratch,
        compiler_params=pltpu.CompilerParams(vmem_limit_bytes=VMEM_LIMIT),
    )(*args)


def shape(*dims, dtype=F32):
    return jax.ShapeDtypeStruct(dims, dtype)


def shards(tiles, cell_slot, counts, src_points, tgt_points):
    help_index = lax.axis_index("help")
    src_index = lax.axis_index("src")
    z, x = help_index // SIDE, help_index % SIDE
    scale = LOG2E / (math.sqrt(WIDTH) * EPSILON)

    positions = jnp.arange(SIDE * PART, dtype=jnp.int32)[:, None]
    marked_src = jnp.where(positions < counts[0, 0], src_points, jnp.asarray(MARK, BF16))
    marked_tgt = jnp.where(positions < counts[0, 1], tgt_points, jnp.asarray(-MARK, BF16))
    tgt_block = spread(marked_tgt, x_perm, x)
    src_block = spread(marked_src, z_perm, z)
    own = collect(tgt_block, z_perm)
    following = [
        (SIDE * SIDE * PART + start, rows, to_group(array, -1)) for start, rows, array in own
    ]
    sources = collect(src_block, x_perm)
    targets_all = own + following
    places_s = tuple((start, rows) for start, rows, _ in sources)
    places_t = tuple((start, rows) for start, rows, _ in targets_all)
    s_arrays = [array for _, _, array in sources]
    t_arrays = [array for _, _, array in targets_all]

    half_src = (0.5 * scale) * jnp.sum(jnp.square(src_points.astype(F32)), axis=1).reshape(SIDE, PART)
    half_tgt = (0.5 * scale) * jnp.sum(jnp.square(tgt_points.astype(F32)), axis=1).reshape(SIDE, PART)

    src_slot = lookup(tiles[0], cell_slot[0])
    tgt_slot = lookup(tiles[1], cell_slot[1])
    src_local = src_slot % SRC_CELLS
    tgt_local = tgt_slot % SRC_CELLS + jnp.where(tgt_slot // SRC_CELLS == src_index, 0, SRC_CELLS)
    keys = src_local * TGT_CELLS + tgt_local
    ranks = jnp.sum((keys[None, :] < keys[:, None]).astype(jnp.int32), axis=1)
    hits = ranks[None, :] == jnp.arange(PAIRS, dtype=jnp.int32)[:, None]
    targets = jnp.sum(jnp.where(hits, tgt_local[None, :], 0), axis=1)
    starts = jnp.sum(
        (src_local[None, :] < jnp.arange(SRC_CELLS + 1, dtype=jnp.int32)[:, None]).astype(jnp.int32), axis=1
    )
    local = jnp.arange(SRC_CELLS, dtype=jnp.int32)
    s_order = (z - local % SIDE) % SIDE * SIDE + (x - local // SIDE) % SIDE
    t_order = (z - local // SIDE) % SIDE * SIDE + (x - local % SIDE) % SIDE

    sums, small = shape(SRC_CELLS, PART), shape(TGT_CELLS, PART)
    table, row_part, first_level, live = call(
        functools.partial(first_kernel, places_s, places_t, scale),
        (shape(PAIRS, PART, PART), sums, small, sums),
        [SM] * 4 + [ANY] * (len(s_arrays) + len(t_arrays)),
        [
            pltpu.VMEM((SRC_CELLS * PART, WIDTH), BF16),
            pltpu.VMEM((TGT_CELLS * PART, WIDTH), BF16),
            pltpu.SemaphoreType.DMA((SRC_CELLS,)),
            pltpu.SemaphoreType.DMA((TGT_CELLS,)),
        ],
        starts,
        targets,
        s_order,
        t_order,
        *s_arrays,
        *t_arrays,
    )
    for sweep in range(ITERS):
        if sweep:
            row_part, _ = call(
                row_kernel,
                (sums, small),
                [SM, SM] + [VM] * 5,
                [],
                starts,
                targets,
                joined,
                before,
                after,
                first_level,
                table,
            )
        col_part, src_level = call(
            column_kernel,
            (small, sums),
            [SM, SM] + [VM] * 6,
            [pltpu.VMEM((TGT_CELLS, 8, PART), F32), pltpu.VMEM((TGT_CELLS, 8, PART), F32)],
            starts,
            targets,
            *ring_parts(row_part, x_perm),
            live,
            table,
        )
        joined = join(ring_parts(col_part, z_perm))
        before = to_group(joined[SRC_CELLS:], 1)
        after = to_group(joined[:SRC_CELLS], -1)
    blocks = call(
        functools.partial(transport_kernel, places_t),
        shape(SRC_CELLS, PART + TAIL, WIDTH, dtype=BF16),
        [SM, SM, SM] + [VM] * 6 + [ANY] * len(t_arrays),
        [
            pltpu.VMEM((TGT_CELLS * PART, WIDTH), BF16),
            pltpu.VMEM((TGT_CELLS, PART), F32),
            pltpu.VMEM((PART, WIDTH), F32),
            pltpu.SemaphoreType.DMA((TGT_CELLS,)),
        ],
        starts,
        targets,
        t_order,
        joined,
        before,
        after,
        first_level,
        src_level,
        table,
        *t_arrays,
    )
    got = lax.all_to_all(blocks, "help", 0, 0)
    source_out, target_out, transport = call(
        finish_kernel,
        (shape(SIDE, PART), shape(SIDE, PART), shape(SIDE * PART, WIDTH)),
        [SM] + [VM] * 3,
        [],
        counts,
        got,
        half_src,
        half_tgt,
    )
    return (source_out.reshape(-1), target_out.reshape(-1), transport)


def solution(mesh):
    in_specs = (
        P(None, "src"),
        P(),
        P(("src", "help"), None),
        P(("src", "help"), None),
        P(("src", "help"), None),
    )
    out_specs = (P(("src", "help")), P(("src", "help")), P(("src", "help"), None))
    return jax.shard_map(shards, mesh=mesh, in_specs=in_specs, out_specs=out_specs, check_vma=False)
```

```python
import functools
import math

import jax
import jax.numpy as jnp
from jax import lax
from jax.experimental import pallas as pl
from jax.experimental.pallas import tpu as pltpu
from jax.sharding import PartitionSpec as P

ITERS = 2
EPSILON = 0.2
LOG2E = 1.0 / math.log(2.0)
DEAD = -1e30
EMPTY = -2e30
MARK = 1024.0
SIDE = 4
PART = 128
WIDTH = 512
SRC_CELLS = 16
TGT_CELLS = 32
TAIL = 16
PAIRS = 128
BATCH = 4
BATCHES = (PAIRS + (BATCH - 1) * SRC_CELLS) // BATCH
STEPS = (BATCHES + 1) // 2
NOBODY = TGT_CELLS
LEVELS = 40
F32 = jnp.float32
BF16 = jnp.bfloat16
VMEM_LIMIT = 48 * 1024 * 1024


def x_perm(by):
    return [(z * SIDE + x, z * SIDE + (x + by) % SIDE) for z in range(SIDE) for x in range(SIDE)]


def z_perm(by):
    return [(z * SIDE + x, (z + by) % SIDE * SIDE + x) for z in range(SIDE) for x in range(SIDE)]


def to_group(array, by):
    count = lax.axis_size("src")
    return lax.ppermute(array, "src", [(i, (i + by) % count) for i in range(count)])


def to_help(array, perm):
    return lax.ppermute(array, "help", perm)


def lookup(cell_ids, slot_table):
    matches = cell_ids[:, None] == jnp.arange(slot_table.shape[0], dtype=jnp.int32)[None, :]
    return jnp.sum(jnp.where(matches, slot_table[None, :], 0), axis=1)


def spread(points, perm, me):
    parts = [lax.dynamic_slice_in_dim(points, me * PART, PART, 0)]
    for by in range(1, SIDE):
        other = (me + by) % SIDE
        parts.append(to_help(lax.dynamic_slice_in_dim(points, other * PART, PART, 0), perm(by)))
    return jnp.concatenate(parts, axis=0)


def collect(block, perm):
    rows = block.shape[0]
    half = rows // 2
    behind = to_help(block, perm(1))
    ahead = to_help(block, perm(SIDE - 1))
    far_low = to_help(behind[:half], perm(1))
    far_high = to_help(ahead[half:], perm(SIDE - 1))
    return [
        (0, rows, block),
        (rows, rows, behind),
        (3 * rows, rows, ahead),
        (2 * rows, half, far_low),
        (2 * rows + half, half, far_high),
    ]


def ring_parts(array, perm):
    return [array] + [to_help(array, perm(by)) for by in range(1, SIDE)]


def join(parts):
    top = functools.reduce(jnp.maximum, parts)
    total = functools.reduce(jnp.add, [jnp.exp2(part - top) for part in parts])
    return top + jnp.log2(total)


def eye():
    return lax.broadcasted_iota(jnp.int32, (PART, PART), 0) == lax.broadcasted_iota(
        jnp.int32, (PART, PART), 1
    )


def to_lanes(column):
    return jnp.sum(jnp.where(eye(), jnp.broadcast_to(column, (PART, PART)), 0.0), axis=0, keepdims=True)


def to_rows(lane_vector):
    return jnp.transpose(jnp.broadcast_to(lane_vector, (PART, PART)))


def part_of(index):
    return pl.ds(pl.multiple_of(index * PART, PART), PART)


def load_blocks(refs, places, order, target, sem):
    copies = []
    for (start, rows), ref in zip(places, refs):
        for cell in range(rows // PART):
            place = start // PART + cell
            side, place = place // SRC_CELLS, place % SRC_CELLS
            goal = part_of(side * SRC_CELLS + order[place])
            copies.append(
                pltpu.make_async_copy(
                    ref.at[pl.ds(cell * PART, PART)], target.at[goal], sem.at[len(copies)]
                )
            )
    for copy in copies:
        copy.start()
    return list(enumerate(copies))


def batch_targets(entries, b):
    return [entries[b * BATCH + k] for k in range(BATCH)]


def tile(k):
    return slice(k * PART, (k + 1) * PART)


def row_stats(scores, s, tops, totals):
    old = tops[s]
    top = functools.reduce(jnp.maximum, scores, old)
    total = functools.reduce(jnp.add, [jnp.exp2(one - top) for one in scores])
    totals[s] = totals[s] * jnp.exp2(old - top) + total
    tops[s] = top


def clear_stats(tops, totals):
    for one in tops:
        one[...] = jnp.full(one.shape, EMPTY, F32)
    for one in totals:
        one[...] = jnp.ones(one.shape, F32)


def store_row_sums(tops, totals, sums_ref):
    def cell(s, carry):
        top = jnp.max(jnp.maximum(tops[0][s], tops[1][s]), axis=1, keepdims=True)
        total = totals[0][s] * jnp.exp2(tops[0][s] - top) + totals[1][s] * jnp.exp2(tops[1][s] - top)
        total = jnp.sum(total, axis=1, keepdims=True)
        sums_ref[pl.ds(s, 1), :] = to_lanes(top + jnp.log2(total))
        return carry

    lax.fori_loop(0, SRC_CELLS, cell, 0, unroll=4)


def table_copy(kept, table, sem, step, out=False):
    ends = (table.at[step], kept.at[step])
    return pltpu.make_async_copy(*(ends if out else ends[::-1]), sem.at[step])


def start_table(kept, table, sem, steps):
    def one(step, carry):
        table_copy(kept, table, sem, step).start()
        return carry

    lax.fori_loop(0, steps, one, 0)


def first_kernel(places_s, places_t, scale, entries, batches, s_order, t_order, *refs):
    ns, nt = len(places_s), len(places_t)
    s_refs, t_refs = refs[:ns], refs[ns : ns + nt]
    kept, sums_ref, first_ref, live_ref = refs[ns + nt : ns + nt + 4]
    xs, ys, level_ref, top0, top1, total0, total1, table, s_sem, t_sem, sem = refs[ns + nt + 4 :]
    tops, totals = (top0, top1), (total0, total1)
    s_copies = load_blocks(s_refs, places_s, s_order, xs, s_sem)
    t_copies = load_blocks(t_refs, places_t, t_order, ys, t_sem)
    steps = batches[0]
    clear_stats(tops, totals)
    level_ref[...] = jnp.full(level_ref.shape, DEAD, F32)
    for place, copy in s_copies:
        copy.wait()
    for place, copy in t_copies:
        copy.wait()

    def target_cell(t, carry):
        points = ys[part_of(t), :].astype(F32)
        half = to_lanes(jnp.sum(points * points, axis=1, keepdims=True)) * (0.5 * scale)
        level_ref[pl.ds(t, 1), :] = jnp.where(half > 1e7, DEAD, -half)
        return carry

    lax.fori_loop(0, TGT_CELLS, target_cell, 0, unroll=4)
    first_ref[...] = level_ref[:TGT_CELLS, :]

    def source_cell(s, carry):
        mark = xs[part_of(s), :PART].astype(F32)
        dead = jnp.where(eye() & (mark > 0.5 * MARK), DEAD, 0.0)
        live_ref[pl.ds(s, 1), :] = jnp.sum(dead, axis=0, keepdims=True)
        return carry

    lax.fori_loop(0, SRC_CELLS, source_cell, 0, unroll=4)

    def step(i, carry):
        for half in range(2):
            b = 2 * i + half
            near = batch_targets(entries, b)
            points = jnp.concatenate([ys[part_of(lax.rem(t, NOBODY)), :] for t in near], axis=0)
            s = batches[1 + b]
            inner = lax.dot_general(
                xs[part_of(s), :], points, (((1,), (1,)), ((), ())), preferred_element_type=F32
            )
            inner = inner * scale
            table[i, half] = inner
            scores = [inner[:, tile(k)] + level_ref[pl.ds(t, 1), :] for k, t in enumerate(near)]
            row_stats(scores, s, tops[half], totals[half])
        table_copy(kept, table, sem, i, out=True).start()
        return carry

    lax.fori_loop(0, steps, step, 0)
    store_row_sums(tops, totals, sums_ref)

    def settle(i, carry):
        table_copy(kept, table, sem, i, out=True).wait()
        return carry

    lax.fori_loop(0, steps, settle, 0)


def source_levels(parts, live):
    return jnp.where(live < 0.5 * DEAD, DEAD, -join([part[...] for part in parts]))


def spread_rows(level_ref, wide_ref):
    def cell(s, carry):
        wide_ref[s] = to_rows(level_ref[pl.ds(s, 1), :])
        return carry

    lax.fori_loop(0, SRC_CELLS, cell, 0, unroll=4)


def column_kernel(
    entries, batches, r0, r1, r2, r3, live_ref, kept, sums_ref, level_ref, top0, top1, total0, total1, wide_ref, table, sem
):
    tops, totals = (top0, top1), (total0, total1)
    steps = batches[0]
    start_table(kept, table, sem, steps)
    level_ref[...] = source_levels((r0, r1, r2, r3), live_ref[...])
    spread_rows(level_ref, wide_ref)
    clear_stats(tops, totals)

    def step(i, carry):
        table_copy(kept, table, sem, i).wait()
        for half in range(2):
            b = 2 * i + half
            near = batch_targets(entries, b)
            level = wide_ref[batches[1 + b]]
            old = [(tops[half][t], totals[half][t]) for t in near]
            new = []
            for k, (old_top, old_total) in enumerate(old):
                scores = (table[i, half, :, tile(k)] + level).reshape(PART // 8, 8, PART)
                top = jnp.maximum(old_top, jnp.max(scores, axis=0))
                total = jnp.sum(jnp.exp2(scores - top[None]), axis=0)
                new.append((top, old_total * jnp.exp2(old_top - top) + total))
            for t, (top, total) in zip(near, new):
                tops[half][t] = top
                totals[half][t] = total
        return carry

    lax.fori_loop(0, steps, step, 0)
    tops = [one[:TGT_CELLS] for one in tops]
    top = jnp.max(jnp.maximum(*tops), axis=1)
    total = sum(kept_total[:TGT_CELLS] * jnp.exp2(one - top[:, None, :]) for one, kept_total in zip(tops, totals))
    sums_ref[...] = top + jnp.log2(jnp.sum(total, axis=1))


def target_levels(joined, before, after, first_level):
    own = -join([joined[:SRC_CELLS], before])
    following = -join([joined[SRC_CELLS:], after])
    levels = jnp.concatenate([own, following], axis=0)
    return jnp.where(first_level < 0.5 * DEAD, DEAD, levels)


def row_kernel(
    entries, batches, joined, before, after, first_level, kept, sums_ref, level_ref, top0, top1, total0, total1, table, sem
):
    tops, totals = (top0, top1), (total0, total1)
    steps = batches[0]
    start_table(kept, table, sem, steps)
    level_ref[:TGT_CELLS, :] = target_levels(joined[...], before[...], after[...], first_level[...])
    level_ref[TGT_CELLS:, :] = jnp.full((LEVELS - TGT_CELLS, PART), DEAD, F32)
    clear_stats(tops, totals)

    def step(i, carry):
        table_copy(kept, table, sem, i).wait()
        for half in range(2):
            b = 2 * i + half
            near = batch_targets(entries, b)
            scores = [table[i, half, :, tile(k)] + level_ref[pl.ds(t, 1), :] for k, t in enumerate(near)]
            row_stats(scores, batches[1 + b], tops[half], totals[half])
        return carry

    lax.fori_loop(0, steps, step, 0)
    store_row_sums(tops, totals, sums_ref)


def pieces(value, count):
    found = []
    for _ in range(count):
        piece = value.astype(BF16).astype(F32)
        found.append(piece)
        value = value - piece
    return found


def transport_kernel(
    places_t, entries, batches, t_order, joined, before, after, first_level, src_level, kept, *refs
):
    nt = len(places_t)
    t_refs = refs[:nt]
    out_ref, ys, level_ref, wide_ref, map0, map1, mass0, mass1, table, t_sem, sem = refs[nt:]
    maps, masses = (map0, map1), (mass0, mass1)
    steps = batches[0]
    copies = load_blocks(t_refs, places_t, t_order, ys, t_sem)
    start_table(kept, table, sem, steps)
    level_ref[:TGT_CELLS, :] = target_levels(joined[...], before[...], after[...], first_level[...])
    level_ref[TGT_CELLS:, :] = jnp.full((LEVELS - TGT_CELLS, PART), DEAD, F32)
    spread_rows(src_level, wide_ref)
    for one in maps + masses:
        one[...] = jnp.zeros(one.shape, F32)
    for place, copy in copies:
        copy.wait()

    def step(i, carry):
        table_copy(kept, table, sem, i).wait()
        for half in range(2):
            b = 2 * i + half
            near = batch_targets(entries, b)
            s = batches[1 + b]
            level = wide_ref[s]
            weights = [
                jnp.exp2(table[i, half, :, tile(k)] + level_ref[pl.ds(t, 1), :] + level).astype(BF16)
                for k, t in enumerate(near)
            ]
            points = jnp.concatenate([ys[part_of(lax.rem(t, NOBODY)), :] for t in near], axis=0)
            maps[half][s] += jnp.dot(jnp.concatenate(weights, axis=1), points, preferred_element_type=F32)
            masses[half][s] += functools.reduce(jnp.add, [one.astype(F32) for one in weights])
        return carry

    lax.fori_loop(0, steps, step, 0)
    rows = lax.broadcasted_iota(jnp.int32, (TAIL, WIDTH), 0)

    def cell(s, carry):
        mass = to_lanes(jnp.sum(mass0[s] + mass1[s], axis=1, keepdims=True))
        out_ref[s, :PART, :] = (map0[s] + map1[s]).astype(BF16)
        parts = pieces(mass, 2) + pieces(src_level[pl.ds(s, 1), :], 3) + pieces(level_ref[pl.ds(s, 1), :], 3)
        tail = jnp.where(
            rows == 0,
            jnp.concatenate(parts[:4], axis=1),
            jnp.where(rows == 1, jnp.concatenate(parts[4:], axis=1), 0.0),
        )
        out_ref[s, PART:, :] = tail.astype(BF16)
        return carry

    lax.fori_loop(0, SRC_CELLS, cell, 0, unroll=2)


def finish_kernel(counts, got, half_src, half_tgt, src_ref, tgt_ref, map_ref):
    def tail(sender):
        return got[sender, PART:, :].astype(F32)

    def segment(rows, index):
        return rows[index // SIDE : index // SIDE + 1, index % SIDE * PART : (index % SIDE + 1) * PART]

    lanes = lax.broadcasted_iota(jnp.int32, (1, PART), 1)
    rows = lax.broadcasted_iota(jnp.int32, (PART, 1), 0)
    src_live, tgt_live = counts[0, 0], counts[0, 1]
    for q in range(SIDE):
        tails = [tail(q * SIDE + x) for x in range(SIDE)]
        weight_sum = sum(segment(one, 0) + segment(one, 1) for one in tails)
        live = rows + q * PART < src_live
        inverse = jnp.where(live, 1.0 / to_rows(weight_sum), 0.0)
        for chunk in range(WIDTH // PART):
            columns = slice(chunk * PART, (chunk + 1) * PART)
            numerator = sum(got[q * SIDE + x, :PART, columns].astype(F32) for x in range(SIDE))
            map_ref[q * PART : (q + 1) * PART, columns] = jnp.where(live, numerator * inverse, 0.0)
        level = segment(tails[0], 2) + segment(tails[0], 3) + segment(tails[0], 4)
        value = (level + half_src[q : q + 1, :]) * (EPSILON / LOG2E)
        src_ref[q : q + 1, :] = jnp.where(lanes + q * PART < src_live, value, 0.0)
        first = tail(q)
        level = segment(first, 5) + segment(first, 6) + segment(first, 7)
        value = (level + half_tgt[q : q + 1, :]) * (EPSILON / LOG2E)
        tgt_ref[q : q + 1, :] = jnp.where(lanes + q * PART < tgt_live, value, 0.0)


VM = pl.BlockSpec(memory_space=pltpu.VMEM)
SM = pl.BlockSpec(memory_space=pltpu.SMEM)
ANY = pl.BlockSpec(memory_space=pl.ANY)


def call(kernel, out_shape, in_specs, scratch, *args, out_specs=None):
    outs = jax.tree.map(lambda _: VM, out_shape) if out_specs is None else out_specs
    return pl.pallas_call(
        kernel,
        out_shape=out_shape,
        in_specs=in_specs,
        out_specs=outs,
        scratch_shapes=scratch,
        compiler_params=pltpu.CompilerParams(vmem_limit_bytes=VMEM_LIMIT),
    )(*args)


def shape(*dims, dtype=F32):
    return jax.ShapeDtypeStruct(dims, dtype)


def shards(tiles, cell_slot, counts, src_points, tgt_points):
    help_index = lax.axis_index("help")
    src_index = lax.axis_index("src")
    z, x = help_index // SIDE, help_index % SIDE
    scale = LOG2E / (math.sqrt(WIDTH) * EPSILON)

    positions = jnp.arange(SIDE * PART, dtype=jnp.int32)[:, None]
    marked_src = jnp.where(positions < counts[0, 0], src_points, jnp.asarray(MARK, BF16))
    marked_tgt = jnp.where(positions < counts[0, 1], tgt_points, jnp.asarray(-MARK, BF16))
    tgt_block = spread(marked_tgt, x_perm, x)
    src_block = spread(marked_src, z_perm, z)
    own = collect(tgt_block, z_perm)
    following = [
        (SIDE * SIDE * PART + start, rows, to_group(array, -1)) for start, rows, array in own
    ]
    sources = collect(src_block, x_perm)
    targets_all = own + following
    places_s = tuple((start, rows) for start, rows, _ in sources)
    places_t = tuple((start, rows) for start, rows, _ in targets_all)
    s_arrays = [array for _, _, array in sources]
    t_arrays = [array for _, _, array in targets_all]

    half_src = (0.5 * scale) * jnp.sum(jnp.square(src_points.astype(F32)), axis=1).reshape(SIDE, PART)
    half_tgt = (0.5 * scale) * jnp.sum(jnp.square(tgt_points.astype(F32)), axis=1).reshape(SIDE, PART)

    src_slot = lookup(tiles[0], cell_slot[0])
    tgt_slot = lookup(tiles[1], cell_slot[1])
    src_local = src_slot % SRC_CELLS
    tgt_local = tgt_slot % SRC_CELLS + jnp.where(tgt_slot // SRC_CELLS == src_index, 0, SRC_CELLS)
    same = src_local[None, :] == src_local[:, None]
    earlier = jnp.arange(PAIRS)[None, :] < jnp.arange(PAIRS)[:, None]
    rank = jnp.sum((same & earlier).astype(jnp.int32), axis=1)
    cells = jnp.arange(SRC_CELLS, dtype=jnp.int32)
    listed = jnp.sum((src_local[None, :] == cells[:, None]).astype(jnp.int32), axis=1)
    used = (listed + (BATCH - 1)) // BATCH
    ends = jnp.sum(jnp.where(cells[None, :] <= cells[:, None], used[None, :], 0), axis=1)
    begins = ends - used
    begin_of = jnp.sum(jnp.where(src_local[:, None] == cells[None, :], begins[None, :], 0), axis=1)
    place = begin_of * BATCH + rank
    hits = place[None, :] == jnp.arange(2 * STEPS * BATCH, dtype=jnp.int32)[:, None]
    entries = jnp.sum(jnp.where(hits, tgt_local[None, :] - NOBODY, 0), axis=1) + NOBODY
    numbers = jnp.arange(2 * STEPS, dtype=jnp.int32)
    batch_src = jnp.sum((ends[None, :] <= numbers[:, None]).astype(jnp.int32), axis=1)
    batch_src = jnp.minimum(batch_src, SRC_CELLS - 1)
    batches = jnp.concatenate([(ends[-1:] + 1) // 2, batch_src])
    local = jnp.arange(SRC_CELLS, dtype=jnp.int32)
    s_order = (z - local % SIDE) % SIDE * SIDE + (x - local // SIDE) % SIDE
    t_order = (z - local // SIDE) % SIDE * SIDE + (x - local % SIDE) % SIDE

    sums, small = shape(SRC_CELLS, PART), shape(TGT_CELLS, PART)
    levels = pltpu.VMEM((LEVELS, PART), F32)
    wide = pltpu.VMEM((SRC_CELLS, PART, PART), F32)
    narrow = pltpu.VMEM((TGT_CELLS + 1, 8, PART), F32)
    table_dims = (STEPS, 2, PART, BATCH * PART)
    table = [pltpu.VMEM(table_dims, F32)]
    table_sem = [pltpu.SemaphoreType.DMA((STEPS,))]
    t_sem = [pltpu.SemaphoreType.DMA((TGT_CELLS,))]
    kept, row_part, first_level, live = call(
        functools.partial(first_kernel, places_s, places_t, scale),
        (shape(*table_dims), sums, small, sums),
        [SM] * 4 + [ANY] * (len(s_arrays) + len(t_arrays)),
        [
            pltpu.VMEM((SRC_CELLS * PART, WIDTH), BF16),
            pltpu.VMEM((TGT_CELLS * PART, WIDTH), BF16),
            levels,
        ]
        + [wide] * 4
        + table
        + [pltpu.SemaphoreType.DMA((SRC_CELLS,))]
        + t_sem
        + table_sem,
        entries,
        batches,
        s_order,
        t_order,
        *s_arrays,
        *t_arrays,
        out_specs=(ANY, VM, VM, VM),
    )
    for sweep in range(ITERS):
        if sweep:
            row_part, _ = call(
                row_kernel,
                (sums, shape(LEVELS, PART)),
                [SM, SM] + [VM] * 4 + [ANY],
                [wide] * 4 + table + table_sem,
                entries,
                batches,
                joined,
                before,
                after,
                first_level,
                kept,
            )
        col_part, src_level = call(
            column_kernel,
            (small, sums),
            [SM, SM] + [VM] * 5 + [ANY],
            [narrow] * 4 + [wide] + table + table_sem,
            entries,
            batches,
            *ring_parts(row_part, x_perm),
            live,
            kept,
        )
        joined = join(ring_parts(col_part, z_perm))
        before = to_group(joined[SRC_CELLS:], 1)
        after = to_group(joined[:SRC_CELLS], -1)
    blocks = call(
        functools.partial(transport_kernel, places_t),
        shape(SRC_CELLS, PART + TAIL, WIDTH, dtype=BF16),
        [SM] * 3 + [VM] * 5 + [ANY] * (1 + len(t_arrays)),
        [pltpu.VMEM((TGT_CELLS * PART, WIDTH), BF16), levels, wide]
        + [pltpu.VMEM((SRC_CELLS, PART, WIDTH), F32)] * 2
        + [wide] * 2
        + table
        + t_sem
        + table_sem,
        entries,
        batches,
        t_order,
        joined,
        before,
        after,
        first_level,
        src_level,
        kept,
        *t_arrays,
    )
    got = lax.all_to_all(blocks, "help", 0, 0)
    source_out, target_out, transport = call(
        finish_kernel,
        (shape(SIDE, PART), shape(SIDE, PART), shape(SIDE * PART, WIDTH)),
        [SM] + [VM] * 3,
        [],
        counts,
        got,
        half_src,
        half_tgt,
    )
    return (source_out.reshape(-1), target_out.reshape(-1), transport)


def solution(mesh):
    in_specs = (
        P(None, "src"),
        P(),
        P(("src", "help"), None),
        P(("src", "help"), None),
        P(("src", "help"), None),
    )
    out_specs = (P(("src", "help")), P(("src", "help")), P(("src", "help"), None))
    return jax.shard_map(shards, mesh=mesh, in_specs=in_specs, out_specs=out_specs, check_vma=False)
```

```python
import functools
import math

import jax
import jax.numpy as jnp
from jax import lax
from jax.experimental import pallas as pl
from jax.experimental.pallas import tpu as pltpu
from jax.sharding import PartitionSpec as P

ITERS = 2
EPSILON = 0.2
LOG2E = 1.0 / math.log(2.0)
DEAD = -1e30
EMPTY = -2e30
MARK = 1024.0
SIDE = 4
PART = 128
WIDTH = 512
SRC_CELLS = 16
TGT_CELLS = 8
TILES = WIDTH // PART
LEVELS = TGT_CELLS * TILES
TAIL = 16
PAIRS = 128
STEPS = PAIRS // 2
RING = 20
NOBODY = TGT_CELLS
F32 = jnp.float32
BF16 = jnp.bfloat16
VMEM_LIMIT = 40 * 1024 * 1024


def x_perm(by):
    return [(z * SIDE + x, z * SIDE + (x + by) % SIDE) for z in range(SIDE) for x in range(SIDE)]


def z_perm(by):
    return [(z * SIDE + x, (z + by) % SIDE * SIDE + x) for z in range(SIDE) for x in range(SIDE)]


def to_group(array, by):
    count = lax.axis_size("src")
    return lax.ppermute(array, "src", [(i, (i + by) % count) for i in range(count)])


def to_help(array, perm):
    return lax.ppermute(array, "help", perm)


def lookup(cell_ids, slot_table):
    matches = cell_ids[:, None] == jnp.arange(slot_table.shape[0], dtype=jnp.int32)[None, :]
    return jnp.sum(jnp.where(matches, slot_table[None, :], 0), axis=1)


def spread(points, perm, me):
    parts = [lax.dynamic_slice_in_dim(points, me * PART, PART, 0)]
    for by in range(1, SIDE):
        other = (me + by) % SIDE
        parts.append(to_help(lax.dynamic_slice_in_dim(points, other * PART, PART, 0), perm(by)))
    return jnp.concatenate(parts, axis=0)


def collect(block, perm):
    rows = block.shape[0]
    half = rows // 2
    behind = to_help(block, perm(1))
    ahead = to_help(block, perm(SIDE - 1))
    far_low = to_help(behind[:half], perm(1))
    far_high = to_help(ahead[half:], perm(SIDE - 1))
    return [
        (0, rows, block),
        (rows, rows, behind),
        (3 * rows, rows, ahead),
        (2 * rows, half, far_low),
        (2 * rows + half, half, far_high),
    ]


def ring_parts(array, perm):
    return [array] + [to_help(array, perm(by)) for by in range(1, SIDE)]


def join(parts):
    top = functools.reduce(jnp.maximum, parts)
    total = functools.reduce(jnp.add, [jnp.exp2(part - top) for part in parts])
    return top + jnp.log2(total)


def eye():
    return lax.broadcasted_iota(jnp.int32, (PART, PART), 0) == lax.broadcasted_iota(
        jnp.int32, (PART, PART), 1
    )


def to_lanes(column):
    return jnp.sum(jnp.where(eye(), jnp.broadcast_to(column, (PART, PART)), 0.0), axis=0, keepdims=True)


def to_rows(lane_vector):
    return jnp.transpose(jnp.broadcast_to(lane_vector, (PART, PART)))


def part_of(index):
    return pl.ds(pl.multiple_of(index * PART, PART), PART)


def load_sources(refs, places, order, target, sem):
    copies = []
    for (start, rows), ref in zip(places, refs):
        for cell in range(rows // PART):
            copies.append(
                pltpu.make_async_copy(
                    ref.at[pl.ds(cell * PART, PART)],
                    target.at[part_of(order[start // PART + cell])],
                    sem.at[len(copies)],
                )
            )
    return copies


def load_targets(refs, places, order, target, sem):
    copies = []
    for (start, rows), ref in zip(places, refs):
        side, place = start // WIDTH // SIDE, start // WIDTH % SIDE
        first = (side * SIDE + order[place]) * WIDTH + start % WIDTH
        goal = target.at[pl.ds(pl.multiple_of(first, PART), rows)]
        copies.append(pltpu.make_async_copy(ref, goal, sem.at[len(copies)]))
    return copies


def tile(k):
    return slice(k * PART, (k + 1) * PART)


def cell_rows(t):
    return pl.ds(pl.multiple_of(lax.rem(t, NOBODY) * WIDTH, WIDTH), WIDTH)


def pair(lists, i, half):
    place = 2 * i + half
    return lists[1 + place], lists[1 + PAIRS + place]


def level_rows(level_ref, t):
    return [level_ref[pl.ds(t * TILES + k, 1), :] for k in range(TILES)]


def row_stats(scores, s, tops, totals):
    old = tops[s]
    top = functools.reduce(jnp.maximum, scores, old)
    total = functools.reduce(jnp.add, [jnp.exp2(one - top) for one in scores])
    totals[s] = totals[s] * jnp.exp2(old - top) + total
    tops[s] = top


def clear_stats(tops, totals):
    for one in tops:
        one[...] = jnp.full(one.shape, EMPTY, F32)
    for one in totals:
        one[...] = jnp.ones(one.shape, F32)


def store_row_sums(tops, totals, sums_ref):
    def cell(s, carry):
        top = jnp.max(jnp.maximum(tops[0][s], tops[1][s]), axis=1, keepdims=True)
        total = totals[0][s] * jnp.exp2(tops[0][s] - top) + totals[1][s] * jnp.exp2(tops[1][s] - top)
        total = jnp.sum(total, axis=1, keepdims=True)
        sums_ref[pl.ds(s, 1), :] = to_lanes(top + jnp.log2(total))
        return carry

    lax.fori_loop(0, SRC_CELLS, cell, 0, unroll=4)


def table_copy(kept, ring, sem, step, out=False):
    slot = lax.rem(step, RING)
    ends = (ring.at[slot], kept.at[step])
    return pltpu.make_async_copy(*(ends if out else ends[::-1]), sem.at[slot])


def stream_start(kept, ring, sem, steps):
    for step in range(RING - 1):

        @pl.when(step < steps)
        def _():
            table_copy(kept, ring, sem, step).start()


def stream_step(kept, ring, sem, step, steps):
    table_copy(kept, ring, sem, step).wait()
    ahead = step + RING - 1

    @pl.when(ahead < steps)
    def _():
        table_copy(kept, ring, sem, ahead).start()

    return ring.at[lax.rem(step, RING)]


def first_kernel(places_s, places_t, scale, lists, s_order, t_order, arrived, *refs):
    ns, nt = len(places_s), len(places_t)
    s_refs, t_refs = refs[:ns], refs[ns : ns + nt]
    kept, sums_ref, first_ref, live_ref = refs[ns + nt : ns + nt + 4]
    xs, ys, level_ref, top0, top1, total0, total1, ring, s_sem, t_sem, sem = refs[ns + nt + 4 :]
    tops, totals = (top0, top1), (total0, total1)
    copies = load_targets(t_refs, places_t, t_order, ys, t_sem)
    copies += load_sources(s_refs, places_s, s_order, xs, s_sem)
    for copy in copies:
        copy.start()
    steps = lists[0]
    clear_stats(tops, totals)
    level_ref[LEVELS:, :] = jnp.full((8, PART), DEAD, F32)
    for place in range(TGT_CELLS):
        t = place // SIDE * SIDE + t_order[place % SIDE]
        for k in range(TILES):
            row = place * TILES + k
            level_ref[pl.ds(t * TILES + k, 1), :] = arrived[row : row + 1, :]
    first_ref[...] = level_ref[:LEVELS, :]
    for copy in copies:
        copy.wait()

    def source_cell(s, carry):
        mark = xs[part_of(s), :PART].astype(F32)
        dead = jnp.where(eye() & (mark > 0.5 * MARK), DEAD, 0.0)
        live_ref[pl.ds(s, 1), :] = jnp.sum(dead, axis=0, keepdims=True)
        return carry

    lax.fori_loop(0, SRC_CELLS, source_cell, 0, unroll=4)

    def step(i, carry):
        @pl.when(i >= RING)
        def _():
            table_copy(kept, ring, sem, i - RING, out=True).wait()

        slot = lax.rem(i, RING)
        for half in range(2):
            s, t = pair(lists, i, half)
            inner = lax.dot_general(
                xs[part_of(s), :], ys[cell_rows(t), :], (((1,), (1,)), ((), ())), preferred_element_type=F32
            )
            inner = inner * scale
            ring[slot, half] = inner
            scores = [inner[:, tile(k)] + level for k, level in enumerate(level_rows(level_ref, t))]
            row_stats(scores, s, tops[half], totals[half])
        table_copy(kept, ring, sem, i, out=True).start()
        return carry

    lax.fori_loop(0, steps, step, 0)
    store_row_sums(tops, totals, sums_ref)

    def settle(i, carry):
        table_copy(kept, ring, sem, i, out=True).wait()
        return carry

    lax.fori_loop(jnp.maximum(steps - RING, 0), steps, settle, 0)


def source_levels(parts, live):
    return jnp.where(live < 0.5 * DEAD, DEAD, -join([part[...] for part in parts]))


def spread_rows(level_ref, wide_ref):
    def cell(s, carry):
        wide_ref[s] = to_rows(level_ref[pl.ds(s, 1), :])
        return carry

    lax.fori_loop(0, SRC_CELLS, cell, 0, unroll=4)


def column_kernel(
    lists, r0, r1, r2, r3, live_ref, kept, sums_ref, level_ref, top0, top1, total0, total1, wide_ref, ring, sem
):
    tops, totals = (top0, top1), (total0, total1)
    steps = lists[0]
    stream_start(kept, ring, sem, steps)
    level_ref[...] = source_levels((r0, r1, r2, r3), live_ref[...])
    spread_rows(level_ref, wide_ref)
    clear_stats(tops, totals)

    def step(i, carry):
        table = stream_step(kept, ring, sem, i, steps)
        for half in range(2):
            s, t = pair(lists, i, half)
            level = wide_ref[s]
            old_tops, old_totals = tops[half][t], totals[half][t]
            for k in range(TILES):
                scores = (table[half, :, tile(k)] + level).reshape(PART // 8, 8, PART)
                top = jnp.maximum(old_tops[k], jnp.max(scores, axis=0))
                total = jnp.sum(jnp.exp2(scores - top[None]), axis=0)
                tops[half][t, k] = top
                totals[half][t, k] = old_totals[k] * jnp.exp2(old_tops[k] - top) + total
        return carry

    lax.fori_loop(0, steps, step, 0)
    tops = [one[:TGT_CELLS].reshape(LEVELS, 8, PART) for one in tops]
    totals = [one[:TGT_CELLS].reshape(LEVELS, 8, PART) for one in totals]
    top = jnp.max(jnp.maximum(*tops), axis=1)
    total = sum(part * jnp.exp2(one - top[:, None, :]) for one, part in zip(tops, totals))
    sums_ref[...] = top + jnp.log2(jnp.sum(total, axis=1))


def target_levels(joined, before, after, first_level, level_ref):
    own = -join([joined[: LEVELS // 2, :], before[...]])
    following = -join([joined[LEVELS // 2 :, :], after[...]])
    levels = jnp.concatenate([own, following], axis=0)
    level_ref[:LEVELS, :] = jnp.where(first_level[...] < 0.5 * DEAD, DEAD, levels)
    level_ref[LEVELS:, :] = jnp.full((8, PART), DEAD, F32)


def row_kernel(
    lists, joined, before, after, first_level, kept, sums_ref, level_ref, top0, top1, total0, total1, ring, sem
):
    tops, totals = (top0, top1), (total0, total1)
    steps = lists[0]
    stream_start(kept, ring, sem, steps)
    target_levels(joined, before, after, first_level, level_ref)
    clear_stats(tops, totals)

    def step(i, carry):
        table = stream_step(kept, ring, sem, i, steps)
        for half in range(2):
            s, t = pair(lists, i, half)
            scores = [table[half, :, tile(k)] + level for k, level in enumerate(level_rows(level_ref, t))]
            row_stats(scores, s, tops[half], totals[half])
        return carry

    lax.fori_loop(0, steps, step, 0)
    store_row_sums(tops, totals, sums_ref)


def pieces(value, count):
    found = []
    for _ in range(count):
        piece = value.astype(BF16).astype(F32)
        found.append(piece)
        value = value - piece
    return found


def transport_kernel(
    places_t, lists, t_order, joined, before, after, first_level, src_level, kept, *refs
):
    nt = len(places_t)
    t_refs = refs[:nt]
    out_ref, own_ref, ys, level_ref, wide_ref, map0, map1, mass0, mass1, ring, t_sem, sem = refs[nt:]
    maps, masses = (map0, map1), (mass0, mass1)
    steps = lists[0]
    copies = load_targets(t_refs, places_t, t_order, ys, t_sem)
    for copy in copies:
        copy.start()
    stream_start(kept, ring, sem, steps)
    target_levels(joined, before, after, first_level, level_ref)
    spread_rows(src_level, wide_ref)
    for one in maps + masses:
        one[...] = jnp.zeros(one.shape, F32)
    for k, level in enumerate(level_rows(level_ref, t_order[0])):
        own_ref[k : k + 1, :] = level
    for copy in copies:
        copy.wait()

    def step(i, carry):
        table = stream_step(kept, ring, sem, i, steps)
        for half in range(2):
            s, t = pair(lists, i, half)
            level = wide_ref[s]
            weights = [
                jnp.exp2(table[half, :, tile(k)] + one + level).astype(BF16)
                for k, one in enumerate(level_rows(level_ref, t))
            ]
            maps[half][s] += jnp.dot(
                jnp.concatenate(weights, axis=1), ys[cell_rows(t), :], preferred_element_type=F32
            )
            masses[half][s] += functools.reduce(jnp.add, [one.astype(F32) for one in weights])
        return carry

    lax.fori_loop(0, steps, step, 0)
    rows = lax.broadcasted_iota(jnp.int32, (TAIL, WIDTH), 0)

    def cell(s, carry):
        mass = to_lanes(jnp.sum(mass0[s] + mass1[s], axis=1, keepdims=True))
        out_ref[s, :PART, :] = (map0[s] + map1[s]).astype(BF16)
        parts = pieces(mass, 2) + pieces(src_level[pl.ds(s, 1), :], 3)
        last = jnp.concatenate([parts[4]] * SIDE, axis=1)
        tail = jnp.where(rows == 0, jnp.concatenate(parts[:4], axis=1), jnp.where(rows == 1, last, 0.0))
        out_ref[s, PART:, :] = tail.astype(BF16)
        return carry

    lax.fori_loop(0, SRC_CELLS, cell, 0, unroll=2)


def finish_kernel(counts, got, own_level, half_src, half_tgt, src_ref, tgt_ref, map_ref):
    def tail(sender):
        return got[sender, PART:, :].astype(F32)

    def segment(rows, index):
        return rows[index // SIDE : index // SIDE + 1, index % SIDE * PART : (index % SIDE + 1) * PART]

    lanes = lax.broadcasted_iota(jnp.int32, (1, PART), 1)
    rows = lax.broadcasted_iota(jnp.int32, (PART, 1), 0)
    src_live, tgt_live = counts[0, 0], counts[0, 1]
    for q in range(SIDE):
        tails = [tail(q * SIDE + x) for x in range(SIDE)]
        weight_sum = sum(segment(one, 0) + segment(one, 1) for one in tails)
        live = rows + q * PART < src_live
        inverse = jnp.where(live, 1.0 / to_rows(weight_sum), 0.0)
        for chunk in range(WIDTH // PART):
            columns = slice(chunk * PART, (chunk + 1) * PART)
            numerator = sum(got[q * SIDE + x, :PART, columns].astype(F32) for x in range(SIDE))
            map_ref[q * PART : (q + 1) * PART, columns] = jnp.where(live, numerator * inverse, 0.0)
        level = segment(tails[0], 2) + segment(tails[0], 3) + segment(tails[0], 4)
        value = (level + half_src[q : q + 1, :]) * (EPSILON / LOG2E)
        src_ref[q : q + 1, :] = jnp.where(lanes + q * PART < src_live, value, 0.0)
        value = (own_level[q : q + 1, :] + half_tgt[q : q + 1, :]) * (EPSILON / LOG2E)
        tgt_ref[q : q + 1, :] = jnp.where(lanes + q * PART < tgt_live, value, 0.0)


VM = pl.BlockSpec(memory_space=pltpu.VMEM)
SM = pl.BlockSpec(memory_space=pltpu.SMEM)
ANY = pl.BlockSpec(memory_space=pl.ANY)


def call(kernel, out_shape, in_specs, scratch, *args, out_specs=None):
    outs = jax.tree.map(lambda _: VM, out_shape) if out_specs is None else out_specs
    return pl.pallas_call(
        kernel,
        out_shape=out_shape,
        in_specs=in_specs,
        out_specs=outs,
        scratch_shapes=scratch,
        compiler_params=pltpu.CompilerParams(vmem_limit_bytes=VMEM_LIMIT),
    )(*args)


def shape(*dims, dtype=F32):
    return jax.ShapeDtypeStruct(dims, dtype)


def half_norms(points, scale):
    return (0.5 * scale) * jnp.sum(jnp.square(points.astype(F32)), axis=1)


def shards(tiles, cell_slot, counts, src_points, tgt_points):
    help_index = lax.axis_index("help")
    src_index = lax.axis_index("src")
    z, x = help_index // SIDE, help_index % SIDE
    scale = LOG2E / (math.sqrt(WIDTH) * EPSILON)

    positions = jnp.arange(SIDE * PART, dtype=jnp.int32)[:, None]
    marked_src = jnp.where(positions < counts[0, 0], src_points, jnp.asarray(MARK, BF16))
    marked_tgt = jnp.where(positions < counts[0, 1], tgt_points, jnp.asarray(-MARK, BF16))
    own = collect(marked_tgt, z_perm)
    src_block = spread(marked_src, z_perm, z)
    following = [(SIDE * WIDTH + start, rows, to_group(array, -1)) for start, rows, array in own]
    sources = collect(src_block, x_perm)
    targets_all = own + following
    places_s = tuple((start, rows) for start, rows, _ in sources)
    places_t = tuple((start, rows) for start, rows, _ in targets_all)
    s_arrays = [array for _, _, array in sources]
    t_arrays = [array for _, _, array in targets_all]
    halves = [half_norms(array, scale) for _, _, array in sorted(targets_all, key=lambda one: one[0])]
    halves = jnp.concatenate(halves).reshape(LEVELS, PART)
    arrived = jnp.where(halves > 1e7, DEAD, -halves)

    half_src = half_norms(src_points, scale).reshape(SIDE, PART)
    half_tgt = half_norms(tgt_points, scale).reshape(SIDE, PART)

    src_slot = lookup(tiles[0], cell_slot[0])
    tgt_slot = lookup(tiles[1], cell_slot[1])
    src_cell = src_slot % SRC_CELLS
    tgt_cell = tgt_slot % SRC_CELLS // SIDE + jnp.where(tgt_slot // SRC_CELLS == src_index, 0, SIDE)
    mine = tgt_slot % SIDE == x
    index = jnp.arange(PAIRS, dtype=jnp.int32)
    place = jnp.sum((mine[None, :] & (index[None, :] < index[:, None])).astype(jnp.int32), axis=1)
    hits = mine[None, :] & (place[None, :] == index[:, None])
    pair_src = jnp.sum(jnp.where(hits, src_cell[None, :], 0), axis=1)
    pair_tgt = jnp.sum(jnp.where(hits, tgt_cell[None, :] - NOBODY, 0), axis=1) + NOBODY
    steps = (jnp.sum(mine.astype(jnp.int32)) + 1) // 2
    lists = jnp.concatenate([steps[None], pair_src, pair_tgt])
    local = jnp.arange(SRC_CELLS, dtype=jnp.int32)
    s_order = (z - local % SIDE) % SIDE * SIDE + (x - local // SIDE) % SIDE
    t_order = (z - jnp.arange(SIDE, dtype=jnp.int32)) % SIDE

    sums, small = shape(SRC_CELLS, PART), shape(LEVELS, PART)
    levels = pltpu.VMEM((LEVELS + 8, PART), F32)
    wide = pltpu.VMEM((SRC_CELLS, PART, PART), F32)
    narrow = pltpu.VMEM((TGT_CELLS + 1, TILES, 8, PART), F32)
    ring = [pltpu.VMEM((RING, 2, PART, WIDTH), F32)]
    ring_sem = [pltpu.SemaphoreType.DMA((RING,))]
    t_sem = [pltpu.SemaphoreType.DMA((len(t_arrays),))]
    kept, row_part, first_level, live = call(
        functools.partial(first_kernel, places_s, places_t, scale),
        (shape(STEPS, 2, PART, WIDTH), sums, small, sums),
        [SM] * 3 + [VM] + [ANY] * (len(s_arrays) + len(t_arrays)),
        [
            pltpu.VMEM((SRC_CELLS * PART, WIDTH), BF16),
            pltpu.VMEM((TGT_CELLS * WIDTH, WIDTH), BF16),
            levels,
        ]
        + [wide] * 4
        + ring
        + [pltpu.SemaphoreType.DMA((SRC_CELLS,))]
        + t_sem
        + ring_sem,
        lists,
        s_order,
        t_order,
        arrived,
        *s_arrays,
        *t_arrays,
        out_specs=(ANY, VM, VM, VM),
    )
    for sweep in range(ITERS):
        if sweep:
            row_part = call(
                row_kernel,
                sums,
                [SM] + [VM] * 4 + [ANY],
                [levels] + [wide] * 4 + ring + ring_sem,
                lists,
                joined,
                before,
                after,
                first_level,
                kept,
            )
        col_part, src_level = call(
            column_kernel,
            (small, sums),
            [SM] + [VM] * 5 + [ANY],
            [narrow] * 4 + [wide] + ring + ring_sem,
            lists,
            *ring_parts(row_part, x_perm),
            live,
            kept,
        )
        joined = join(ring_parts(col_part, z_perm))
        before = to_group(joined[LEVELS // 2 :], 1)
        after = to_group(joined[: LEVELS // 2], -1)
    blocks, own_level = call(
        functools.partial(transport_kernel, places_t),
        (shape(SRC_CELLS, PART + TAIL, WIDTH, dtype=BF16), shape(SIDE, PART)),
        [SM] * 2 + [VM] * 5 + [ANY] * (1 + len(t_arrays)),
        [pltpu.VMEM((TGT_CELLS * WIDTH, WIDTH), BF16), levels, wide]
        + [pltpu.VMEM((SRC_CELLS, PART, WIDTH), F32)] * 2
        + [wide] * 2
        + ring
        + t_sem
        + ring_sem,
        lists,
        t_order,
        joined,
        before,
        after,
        first_level,
        src_level,
        kept,
        *t_arrays,
    )
    got = lax.all_to_all(blocks, "help", 0, 0)
    source_out, target_out, transport = call(
        finish_kernel,
        (shape(SIDE, PART), shape(SIDE, PART), shape(SIDE * PART, WIDTH)),
        [SM] + [VM] * 4,
        [],
        counts,
        got,
        own_level,
        half_src,
        half_tgt,
    )
    return (source_out.reshape(-1), target_out.reshape(-1), transport)


def solution(mesh):
    in_specs = (
        P(None, "src"),
        P(),
        P(("src", "help"), None),
        P(("src", "help"), None),
        P(("src", "help"), None),
    )
    out_specs = (P(("src", "help")), P(("src", "help")), P(("src", "help"), None))
    return jax.shard_map(shards, mesh=mesh, in_specs=in_specs, out_specs=out_specs, check_vma=False)
```

```python
import functools
import math

import jax
import jax.numpy as jnp
from jax import lax
from jax.experimental import pallas as pl
from jax.experimental.pallas import tpu as pltpu
from jax.sharding import PartitionSpec as P

ITERS = 2
EPSILON = 0.2
LOG2E = 1.0 / math.log(2.0)
DEAD = -1e30
EMPTY = -2e30
MARK = 1024.0
SIDE = 4
PART = 128
WIDTH = 512
SRC_CELLS = 16
TGT_CELLS = 8
TILES = WIDTH // PART
LEVELS = TGT_CELLS * TILES
TAIL = 16
PAIRS = 128
STEPS = PAIRS // 2
RING = 20
NOBODY = TGT_CELLS
F32 = jnp.float32
BF16 = jnp.bfloat16
VMEM_LIMIT = 40 * 1024 * 1024


def x_perm(by):
    return [(z * SIDE + x, z * SIDE + (x + by) % SIDE) for z in range(SIDE) for x in range(SIDE)]


def z_perm(by):
    return [(z * SIDE + x, (z + by) % SIDE * SIDE + x) for z in range(SIDE) for x in range(SIDE)]


def to_group(array, by):
    count = lax.axis_size("src")
    return lax.ppermute(array, "src", [(i, (i + by) % count) for i in range(count)])


def to_help(array, perm):
    return lax.ppermute(array, "help", perm)


def lookup(cell_ids, slot_table):
    matches = cell_ids[:, None] == jnp.arange(slot_table.shape[0], dtype=jnp.int32)[None, :]
    return jnp.sum(jnp.where(matches, slot_table[None, :], 0), axis=1)


def quarters(points, me):
    return [lax.dynamic_slice_in_dim(points, (me + by) % SIDE * PART, PART, 0) for by in range(SIDE)]


def spread(parts, perm):
    return [part if by == 0 else to_help(part, perm(by)) for by, part in enumerate(parts)]


def collect(block, perm):
    rows = block.shape[0]
    half = rows // 2
    behind = to_help(block, perm(1))
    ahead = to_help(block, perm(SIDE - 1))
    far_low = to_help(behind[:half], perm(1))
    far_high = to_help(ahead[half:], perm(SIDE - 1))
    return [
        (0, rows, block),
        (rows, rows, behind),
        (3 * rows, rows, ahead),
        (2 * rows, half, far_low),
        (2 * rows + half, half, far_high),
    ]


def ring_parts(array, perm):
    return [array] + [to_help(array, perm(by)) for by in range(1, SIDE)]


def join(parts):
    top = functools.reduce(jnp.maximum, parts)
    total = functools.reduce(jnp.add, [jnp.exp2(part - top) for part in parts])
    return top + jnp.log2(total)


def eye():
    return lax.broadcasted_iota(jnp.int32, (PART, PART), 0) == lax.broadcasted_iota(
        jnp.int32, (PART, PART), 1
    )


def to_lanes(column):
    return jnp.sum(jnp.where(eye(), jnp.broadcast_to(column, (PART, PART)), 0.0), axis=0, keepdims=True)


def to_rows(lane_vector):
    return jnp.transpose(jnp.broadcast_to(lane_vector, (PART, PART)))


def part_of(index):
    return pl.ds(pl.multiple_of(index * PART, PART), PART)


def load_sources(refs, places, order, target, sem):
    copies = []
    for (start, rows), ref in zip(places, refs):
        for cell in range(rows // PART):
            copies.append(
                pltpu.make_async_copy(
                    ref.at[pl.ds(cell * PART, PART)],
                    target.at[part_of(order[start // PART + cell])],
                    sem.at[len(copies)],
                )
            )
    return copies


def load_targets(refs, places, order, target, sem):
    copies = []
    for cells, ref in zip(places, refs):
        for index, cell in enumerate(cells):
            side, place = cell // SIDE, cell % SIDE
            copies.append(
                pltpu.make_async_copy(
                    ref.at[pl.ds(index * WIDTH, WIDTH)],
                    target.at[cell_rows(side * SIDE + order[place])],
                    sem.at[len(copies)],
                )
            )
    return copies


def tile(k):
    return slice(k * PART, (k + 1) * PART)


def cell_rows(t):
    return pl.ds(pl.multiple_of(lax.rem(t, NOBODY) * WIDTH, WIDTH), WIDTH)


def pair(lists, i, half):
    place = 2 * i + half
    return lists[1 + place], lists[1 + PAIRS + place]


def level_rows(level_ref, t):
    return [level_ref[pl.ds(t * TILES + k, 1), :] for k in range(TILES)]


def row_stats(scores, s, tops, totals):
    old = tops[s]
    top = functools.reduce(jnp.maximum, scores, old)
    total = functools.reduce(jnp.add, [jnp.exp2(one - top) for one in scores])
    totals[s] = totals[s] * jnp.exp2(old - top) + total
    tops[s] = top


def clear_stats(tops, totals):
    for one in tops:
        one[...] = jnp.full(one.shape, EMPTY, F32)
    for one in totals:
        one[...] = jnp.ones(one.shape, F32)


def store_row_sums(tops, totals, sums_ref):
    def cell(s, carry):
        top = jnp.max(jnp.maximum(tops[0][s], tops[1][s]), axis=1, keepdims=True)
        total = totals[0][s] * jnp.exp2(tops[0][s] - top) + totals[1][s] * jnp.exp2(tops[1][s] - top)
        total = jnp.sum(total, axis=1, keepdims=True)
        sums_ref[pl.ds(s, 1), :] = to_lanes(top + jnp.log2(total))
        return carry

    lax.fori_loop(0, SRC_CELLS, cell, 0, unroll=4)


def table_copy(kept, ring, sem, step, out=False):
    slot = lax.rem(step, RING)
    ends = (ring.at[slot], kept.at[step])
    return pltpu.make_async_copy(*(ends if out else ends[::-1]), sem.at[slot])


def stream_start(kept, ring, sem, steps):
    for step in range(RING - 1):

        @pl.when(step < steps)
        def _():
            table_copy(kept, ring, sem, step).start()


def stream_step(kept, ring, sem, step, steps):
    table_copy(kept, ring, sem, step).wait()
    ahead = step + RING - 1

    @pl.when(ahead < steps)
    def _():
        table_copy(kept, ring, sem, ahead).start()

    return ring.at[lax.rem(step, RING)]


def first_kernel(places_s, places_t, scale, lists, s_order, t_order, arrived, *refs):
    ns, nt = len(places_s), len(places_t)
    s_refs, t_refs = refs[:ns], refs[ns : ns + nt]
    kept, sums_ref, first_ref, live_ref = refs[ns + nt : ns + nt + 4]
    xs, ys, level_ref, top0, top1, total0, total1, ring, s_sem, t_sem, sem = refs[ns + nt + 4 :]
    tops, totals = (top0, top1), (total0, total1)
    copies = load_targets(t_refs, places_t, t_order, ys, t_sem)
    copies += load_sources(s_refs, places_s, s_order, xs, s_sem)
    for copy in copies:
        copy.start()
    steps = lists[0]
    clear_stats(tops, totals)
    level_ref[LEVELS:, :] = jnp.full((8, PART), DEAD, F32)
    for place in range(TGT_CELLS):
        t = place // SIDE * SIDE + t_order[place % SIDE]
        for k in range(TILES):
            row = place * TILES + k
            level_ref[pl.ds(t * TILES + k, 1), :] = arrived[row : row + 1, :]
    first_ref[...] = level_ref[:LEVELS, :]
    for copy in copies:
        copy.wait()

    def source_cell(s, carry):
        mark = xs[part_of(s), :PART].astype(F32)
        dead = jnp.where(eye() & (mark > 0.5 * MARK), DEAD, 0.0)
        live_ref[pl.ds(s, 1), :] = jnp.sum(dead, axis=0, keepdims=True)
        return carry

    lax.fori_loop(0, SRC_CELLS, source_cell, 0, unroll=4)

    def step(i, carry):
        @pl.when(i >= RING)
        def _():
            table_copy(kept, ring, sem, i - RING, out=True).wait()

        slot = lax.rem(i, RING)
        for half in range(2):
            s, t = pair(lists, i, half)
            inner = lax.dot_general(
                xs[part_of(s), :], ys[cell_rows(t), :], (((1,), (1,)), ((), ())), preferred_element_type=F32
            )
            inner = inner * scale
            ring[slot, half] = inner
            scores = [inner[:, tile(k)] + level for k, level in enumerate(level_rows(level_ref, t))]
            row_stats(scores, s, tops[half], totals[half])
        table_copy(kept, ring, sem, i, out=True).start()
        return carry

    lax.fori_loop(0, steps, step, 0)
    store_row_sums(tops, totals, sums_ref)

    def settle(i, carry):
        table_copy(kept, ring, sem, i, out=True).wait()
        return carry

    lax.fori_loop(jnp.maximum(steps - RING, 0), steps, settle, 0)


def source_levels(parts, live):
    return jnp.where(live < 0.5 * DEAD, DEAD, -join([part[...] for part in parts]))


def spread_rows(level_ref, wide_ref):
    def cell(s, carry):
        wide_ref[s] = to_rows(level_ref[pl.ds(s, 1), :])
        return carry

    lax.fori_loop(0, SRC_CELLS, cell, 0, unroll=4)


def column_kernel(
    lists, r0, r1, r2, r3, live_ref, kept, sums_ref, level_ref, top0, top1, total0, total1, wide_ref, ring, sem
):
    tops, totals = (top0, top1), (total0, total1)
    steps = lists[0]
    stream_start(kept, ring, sem, steps)
    level_ref[...] = source_levels((r0, r1, r2, r3), live_ref[...])
    spread_rows(level_ref, wide_ref)
    clear_stats(tops, totals)

    def step(i, carry):
        table = stream_step(kept, ring, sem, i, steps)
        for half in range(2):
            s, t = pair(lists, i, half)
            level = wide_ref[s]
            old_tops, old_totals = tops[half][t], totals[half][t]
            for k in range(TILES):
                scores = (table[half, :, tile(k)] + level).reshape(PART // 8, 8, PART)
                top = jnp.maximum(old_tops[k], jnp.max(scores, axis=0))
                total = jnp.sum(jnp.exp2(scores - top[None]), axis=0)
                tops[half][t, k] = top
                totals[half][t, k] = old_totals[k] * jnp.exp2(old_tops[k] - top) + total
        return carry

    lax.fori_loop(0, steps, step, 0)
    tops = [one[:TGT_CELLS].reshape(LEVELS, 8, PART) for one in tops]
    totals = [one[:TGT_CELLS].reshape(LEVELS, 8, PART) for one in totals]
    top = jnp.max(jnp.maximum(*tops), axis=1)
    total = sum(part * jnp.exp2(one - top[:, None, :]) for one, part in zip(tops, totals))
    sums_ref[...] = top + jnp.log2(jnp.sum(total, axis=1))


def target_levels(joined, before, after, first_level, level_ref):
    own = -join([joined[: LEVELS // 2, :], before[...]])
    following = -join([joined[LEVELS // 2 :, :], after[...]])
    levels = jnp.concatenate([own, following], axis=0)
    level_ref[:LEVELS, :] = jnp.where(first_level[...] < 0.5 * DEAD, DEAD, levels)
    level_ref[LEVELS:, :] = jnp.full((8, PART), DEAD, F32)


def row_kernel(
    lists, joined, before, after, first_level, kept, sums_ref, level_ref, top0, top1, total0, total1, ring, sem
):
    tops, totals = (top0, top1), (total0, total1)
    steps = lists[0]
    stream_start(kept, ring, sem, steps)
    target_levels(joined, before, after, first_level, level_ref)
    clear_stats(tops, totals)

    def step(i, carry):
        table = stream_step(kept, ring, sem, i, steps)
        for half in range(2):
            s, t = pair(lists, i, half)
            scores = [table[half, :, tile(k)] + level for k, level in enumerate(level_rows(level_ref, t))]
            row_stats(scores, s, tops[half], totals[half])
        return carry

    lax.fori_loop(0, steps, step, 0)
    store_row_sums(tops, totals, sums_ref)


def pieces(value, count):
    found = []
    for _ in range(count):
        piece = value.astype(BF16).astype(F32)
        found.append(piece)
        value = value - piece
    return found


def transport_kernel(
    places_t, lists, t_order, joined, before, after, first_level, src_level, kept, *refs
):
    nt = len(places_t)
    t_refs = refs[:nt]
    out_ref, own_ref, ys, level_ref, wide_ref, map0, map1, mass0, mass1, ring, t_sem, sem = refs[nt:]
    maps, masses = (map0, map1), (mass0, mass1)
    steps = lists[0]
    copies = load_targets(t_refs, places_t, t_order, ys, t_sem)
    for copy in copies:
        copy.start()
    stream_start(kept, ring, sem, steps)
    target_levels(joined, before, after, first_level, level_ref)
    spread_rows(src_level, wide_ref)
    for one in maps + masses:
        one[...] = jnp.zeros(one.shape, F32)
    for k, level in enumerate(level_rows(level_ref, t_order[0])):
        own_ref[k : k + 1, :] = level
    for copy in copies:
        copy.wait()

    def step(i, carry):
        table = stream_step(kept, ring, sem, i, steps)
        for half in range(2):
            s, t = pair(lists, i, half)
            level = wide_ref[s]
            weights = [
                jnp.exp2(table[half, :, tile(k)] + one + level).astype(BF16)
                for k, one in enumerate(level_rows(level_ref, t))
            ]
            maps[half][s] += jnp.dot(
                jnp.concatenate(weights, axis=1), ys[cell_rows(t), :], preferred_element_type=F32
            )
            masses[half][s] += functools.reduce(jnp.add, [one.astype(F32) for one in weights])
        return carry

    lax.fori_loop(0, steps, step, 0)
    rows = lax.broadcasted_iota(jnp.int32, (TAIL, WIDTH), 0)

    def cell(s, carry):
        mass = to_lanes(jnp.sum(mass0[s] + mass1[s], axis=1, keepdims=True))
        out_ref[s, :PART, :] = (map0[s] + map1[s]).astype(BF16)
        parts = pieces(mass, 2) + pieces(src_level[pl.ds(s, 1), :], 3)
        last = jnp.concatenate([parts[4]] * SIDE, axis=1)
        tail = jnp.where(rows == 0, jnp.concatenate(parts[:4], axis=1), jnp.where(rows == 1, last, 0.0))
        out_ref[s, PART:, :] = tail.astype(BF16)
        return carry

    lax.fori_loop(0, SRC_CELLS, cell, 0, unroll=2)


def finish_kernel(counts, got, own_level, half_src, half_tgt, src_ref, tgt_ref, map_ref):
    def tail(sender):
        return got[sender, PART:, :].astype(F32)

    def segment(rows, index):
        return rows[index // SIDE : index // SIDE + 1, index % SIDE * PART : (index % SIDE + 1) * PART]

    lanes = lax.broadcasted_iota(jnp.int32, (1, PART), 1)
    rows = lax.broadcasted_iota(jnp.int32, (PART, 1), 0)
    src_live, tgt_live = counts[0, 0], counts[0, 1]
    for q in range(SIDE):
        tails = [tail(q * SIDE + x) for x in range(SIDE)]
        weight_sum = sum(segment(one, 0) + segment(one, 1) for one in tails)
        live = rows + q * PART < src_live
        inverse = jnp.where(live, 1.0 / to_rows(weight_sum), 0.0)
        for chunk in range(WIDTH // PART):
            columns = slice(chunk * PART, (chunk + 1) * PART)
            numerator = sum(got[q * SIDE + x, :PART, columns].astype(F32) for x in range(SIDE))
            map_ref[q * PART : (q + 1) * PART, columns] = jnp.where(live, numerator * inverse, 0.0)
        level = segment(tails[0], 2) + segment(tails[0], 3) + segment(tails[0], 4)
        value = (level + half_src[q : q + 1, :]) * (EPSILON / LOG2E)
        src_ref[q : q + 1, :] = jnp.where(lanes + q * PART < src_live, value, 0.0)
        value = (own_level[q : q + 1, :] + half_tgt[q : q + 1, :]) * (EPSILON / LOG2E)
        tgt_ref[q : q + 1, :] = jnp.where(lanes + q * PART < tgt_live, value, 0.0)


VM = pl.BlockSpec(memory_space=pltpu.VMEM)
SM = pl.BlockSpec(memory_space=pltpu.SMEM)
ANY = pl.BlockSpec(memory_space=pl.ANY)


def call(kernel, out_shape, in_specs, scratch, *args, out_specs=None):
    outs = jax.tree.map(lambda _: VM, out_shape) if out_specs is None else out_specs
    return pl.pallas_call(
        kernel,
        out_shape=out_shape,
        in_specs=in_specs,
        out_specs=outs,
        scratch_shapes=scratch,
        compiler_params=pltpu.CompilerParams(vmem_limit_bytes=VMEM_LIMIT),
    )(*args)


def shape(*dims, dtype=F32):
    return jax.ShapeDtypeStruct(dims, dtype)


def half_norms(points, scale):
    return (0.5 * scale) * jnp.sum(jnp.square(points.astype(F32)), axis=1)


def shards(tiles, cell_slot, counts, src_points, tgt_points):
    help_index = lax.axis_index("help")
    src_index = lax.axis_index("src")
    z, x = help_index // SIDE, help_index % SIDE
    scale = LOG2E / (math.sqrt(WIDTH) * EPSILON)

    positions = jnp.arange(SIDE * PART, dtype=jnp.int32)[:, None]
    marked_src = jnp.where(positions < counts[0, 0], src_points, jnp.asarray(MARK, BF16))
    marked_tgt = jnp.where(positions < counts[0, 1], tgt_points, jnp.asarray(-MARK, BF16))
    next_first = to_group(marked_tgt, -1)
    parts = spread(quarters(marked_src, z), z_perm)
    src_block = jnp.concatenate(parts, axis=0)
    _, later_tgt = lax.optimization_barrier((parts[1], marked_tgt))
    own = collect(later_tgt, z_perm)
    _, tiles, cell_slot = lax.optimization_barrier((own[1][2], tiles, cell_slot))
    around = jnp.concatenate([own[1][2], own[2][2]], axis=0)
    opposite = jnp.concatenate([own[3][2], own[4][2]], axis=0)
    own = [((0,), marked_tgt), ((1, 3), around), ((2,), opposite)]
    following = [((SIDE,), next_first)] + [
        (tuple(SIDE + cell for cell in cells), to_group(array, -1)) for cells, array in own[1:]
    ]
    sources = collect(src_block, x_perm)
    targets_all = own + following
    places_s = tuple((start, rows) for start, rows, _ in sources)
    places_t = tuple(cells for cells, _ in targets_all)
    s_arrays = [array for _, _, array in sources]
    t_arrays = [array for _, array in targets_all]
    halves = [half_norms(array, scale).reshape(-1, TILES, PART) for array in t_arrays]
    halves = [
        part for at in (0, 3) for part in (halves[at], halves[at + 1][:1], halves[at + 2], halves[at + 1][1:])
    ]
    halves = jnp.concatenate(halves).reshape(LEVELS, PART)
    arrived = jnp.where(halves > 1e7, DEAD, -halves)

    src_slot = lookup(tiles[0], cell_slot[0])
    tgt_slot = lookup(tiles[1], cell_slot[1])
    src_cell = src_slot % SRC_CELLS
    tgt_cell = tgt_slot % SRC_CELLS // SIDE + jnp.where(tgt_slot // SRC_CELLS == src_index, 0, SIDE)
    mine = tgt_slot % SIDE == x
    index = jnp.arange(PAIRS, dtype=jnp.int32)
    place = jnp.sum((mine[None, :] & (index[None, :] < index[:, None])).astype(jnp.int32), axis=1)
    hits = mine[None, :] & (place[None, :] == index[:, None])
    pair_src = jnp.sum(jnp.where(hits, src_cell[None, :], 0), axis=1)
    pair_tgt = jnp.sum(jnp.where(hits, tgt_cell[None, :] - NOBODY, 0), axis=1) + NOBODY
    steps = (jnp.sum(mine.astype(jnp.int32)) + 1) // 2
    lists = jnp.concatenate([steps[None], pair_src, pair_tgt])
    local = jnp.arange(SRC_CELLS, dtype=jnp.int32)
    s_order = (z - local % SIDE) % SIDE * SIDE + (x - local // SIDE) % SIDE
    t_order = (z - jnp.arange(SIDE, dtype=jnp.int32)) % SIDE

    sums, small = shape(SRC_CELLS, PART), shape(LEVELS, PART)
    levels = pltpu.VMEM((LEVELS + 8, PART), F32)
    wide = pltpu.VMEM((SRC_CELLS, PART, PART), F32)
    narrow = pltpu.VMEM((TGT_CELLS + 1, TILES, 8, PART), F32)
    ring = [pltpu.VMEM((RING, 2, PART, WIDTH), F32)]
    ring_sem = [pltpu.SemaphoreType.DMA((RING,))]
    t_sem = [pltpu.SemaphoreType.DMA((TGT_CELLS,))]
    kept, row_part, first_level, live = call(
        functools.partial(first_kernel, places_s, places_t, scale),
        (shape(STEPS, 2, PART, WIDTH), sums, small, sums),
        [SM] * 3 + [VM] + [ANY] * (len(s_arrays) + len(t_arrays)),
        [
            pltpu.VMEM((SRC_CELLS * PART, WIDTH), BF16),
            pltpu.VMEM((TGT_CELLS * WIDTH, WIDTH), BF16),
            levels,
        ]
        + [wide] * 4
        + ring
        + [pltpu.SemaphoreType.DMA((SRC_CELLS,))]
        + t_sem
        + ring_sem,
        lists,
        s_order,
        t_order,
        arrived,
        *s_arrays,
        *t_arrays,
        out_specs=(ANY, VM, VM, VM),
    )
    for sweep in range(ITERS):
        if sweep:
            row_part = call(
                row_kernel,
                sums,
                [SM] + [VM] * 4 + [ANY],
                [levels] + [wide] * 4 + ring + ring_sem,
                lists,
                joined,
                before,
                after,
                first_level,
                kept,
            )
        col_part, src_level = call(
            column_kernel,
            (small, sums),
            [SM] + [VM] * 5 + [ANY],
            [narrow] * 4 + [wide] + ring + ring_sem,
            lists,
            *ring_parts(row_part, x_perm),
            live,
            kept,
        )
        joined = join(ring_parts(col_part, z_perm))
        before = to_group(joined[LEVELS // 2 :], 1)
        after = to_group(joined[: LEVELS // 2], -1)
    blocks, own_level = call(
        functools.partial(transport_kernel, places_t),
        (shape(SRC_CELLS, PART + TAIL, WIDTH, dtype=BF16), shape(SIDE, PART)),
        [SM] * 2 + [VM] * 5 + [ANY] * (1 + len(t_arrays)),
        [pltpu.VMEM((TGT_CELLS * WIDTH, WIDTH), BF16), levels, wide]
        + [pltpu.VMEM((SRC_CELLS, PART, WIDTH), F32)] * 2
        + [wide] * 2
        + ring
        + t_sem
        + ring_sem,
        lists,
        t_order,
        joined,
        before,
        after,
        first_level,
        src_level,
        kept,
        *t_arrays,
    )
    got = lax.all_to_all(blocks, "help", 0, 0)
    _, src_after, tgt_after = lax.optimization_barrier((src_level, src_points, tgt_points))
    half_src = half_norms(src_after, scale).reshape(SIDE, PART)
    half_tgt = half_norms(tgt_after, scale).reshape(SIDE, PART)
    source_out, target_out, transport = call(
        finish_kernel,
        (shape(SIDE, PART), shape(SIDE, PART), shape(SIDE * PART, WIDTH)),
        [SM] + [VM] * 4,
        [],
        counts,
        got,
        own_level,
        half_src,
        half_tgt,
    )
    return (source_out.reshape(-1), target_out.reshape(-1), transport)


def solution(mesh):
    in_specs = (
        P(None, "src"),
        P(),
        P(("src", "help"), None),
        P(("src", "help"), None),
        P(("src", "help"), None),
    )
    out_specs = (P(("src", "help")), P(("src", "help")), P(("src", "help"), None))
    return jax.shard_map(shards, mesh=mesh, in_specs=in_specs, out_specs=out_specs, check_vma=False)
```

```python
import functools
import math

import jax
import jax.numpy as jnp
from jax import lax
from jax.experimental import pallas as pl
from jax.experimental.pallas import tpu as pltpu
from jax.sharding import PartitionSpec as P

ITERS = 2
EPSILON = 0.2
LOG2E = 1.0 / math.log(2.0)
DEAD = -1e30
EMPTY = -2e30
MARK = 1024.0
SIDE = 4
PART = 128
WIDTH = 512
SRC_CELLS = 16
TGT_CELLS = 8
TILES = WIDTH // PART
LEVELS = TGT_CELLS * TILES
TAIL = 16
PAIRS = 128
STEPS = PAIRS // 2
RING = 12
NOBODY = TGT_CELLS
F32 = jnp.float32
BF16 = jnp.bfloat16
VMEM_LIMIT = 28 * 1024 * 1024


def x_perm(by):
    return [(z * SIDE + x, z * SIDE + (x + by) % SIDE) for z in range(SIDE) for x in range(SIDE)]


def z_perm(by):
    return [(z * SIDE + x, (z + by) % SIDE * SIDE + x) for z in range(SIDE) for x in range(SIDE)]


def to_group(array, by):
    count = lax.axis_size("src")
    return lax.ppermute(array, "src", [(i, (i + by) % count) for i in range(count)])


def to_help(array, perm):
    return lax.ppermute(array, "help", perm)


def lookup(cell_ids, slot_table):
    matches = cell_ids[:, None] == jnp.arange(slot_table.shape[0], dtype=jnp.int32)[None, :]
    return jnp.sum(jnp.where(matches, slot_table[None, :], 0), axis=1)


def mark_kernel(counts, place, src_ref, tgt_ref, q0, q1, q2, q3, marked_ref):
    rows = lax.broadcasted_iota(jnp.int32, (PART, WIDTH), 0)

    def marked(ref, q, count, mark):
        points = ref[part_of(q), :].astype(F32)
        return jnp.where(rows + q * PART < count, points, mark).astype(BF16)

    for by, out in enumerate((q0, q1, q2, q3)):
        out[...] = marked(src_ref, lax.rem(place[0] + by, SIDE), counts[0, 0], MARK)
    for q in range(SIDE):
        marked_ref[q * PART : (q + 1) * PART, :] = marked(tgt_ref, q, counts[0, 1], -MARK)


def spread(parts, perm):
    return [part if by == 0 else to_help(part, perm(by)) for by, part in enumerate(parts)]


def collect(block, perm):
    rows = block.shape[0]
    half = rows // 2
    behind = to_help(block, perm(1))
    ahead = to_help(block, perm(SIDE - 1))
    far_low = to_help(behind[:half], perm(1))
    far_high = to_help(ahead[half:], perm(SIDE - 1))
    return [
        (0, rows, block),
        (rows, rows, behind),
        (3 * rows, rows, ahead),
        (2 * rows, half, far_low),
        (2 * rows + half, half, far_high),
    ]


def ring_parts(array, perm):
    return [array] + [to_help(array, perm(by)) for by in range(1, SIDE)]


def join(parts):
    top = functools.reduce(jnp.maximum, parts)
    total = functools.reduce(jnp.add, [jnp.exp2(part - top) for part in parts])
    return top + jnp.log2(total)


def eye():
    return lax.broadcasted_iota(jnp.int32, (PART, PART), 0) == lax.broadcasted_iota(
        jnp.int32, (PART, PART), 1
    )


def to_lanes(column):
    return jnp.sum(jnp.where(eye(), jnp.broadcast_to(column, (PART, PART)), 0.0), axis=0, keepdims=True)


def to_rows(lane_vector):
    return jnp.transpose(jnp.broadcast_to(lane_vector, (PART, PART)))


def part_of(index):
    return pl.ds(pl.multiple_of(index * PART, PART), PART)


def load_sources(refs, places, order, target, sem):
    copies = []
    for (start, rows), ref in zip(places, refs):
        for cell in range(rows // PART):
            copies.append(
                pltpu.make_async_copy(
                    ref.at[pl.ds(cell * PART, PART)],
                    target.at[part_of(order[start // PART + cell])],
                    sem.at[len(copies)],
                )
            )
    return copies


def load_targets(refs, places, order, target, sem):
    copies = []
    for cells, ref in zip(places, refs):
        for index, cell in enumerate(cells):
            side, place = cell // SIDE, cell % SIDE
            copies.append(
                pltpu.make_async_copy(
                    ref.at[pl.ds(index * WIDTH, WIDTH)],
                    target.at[cell_rows(side * SIDE + order[place])],
                    sem.at[len(copies)],
                )
            )
    return copies


def tile(k):
    return slice(k * PART, (k + 1) * PART)


def cell_rows(t):
    return pl.ds(pl.multiple_of(lax.rem(t, NOBODY) * WIDTH, WIDTH), WIDTH)


def pair(lists, i, half):
    place = 2 * i + half
    return lists[1 + place], lists[1 + PAIRS + place]


def level_rows(level_ref, t):
    return [level_ref[pl.ds(t * TILES + k, 1), :] for k in range(TILES)]


def row_stats(scores, s, tops, totals):
    old = tops[s]
    top = functools.reduce(jnp.maximum, scores, old)
    total = functools.reduce(jnp.add, [jnp.exp2(one - top) for one in scores])
    totals[s] = totals[s] * jnp.exp2(old - top) + total
    tops[s] = top


def clear_stats(tops, totals):
    for one in tops:
        one[...] = jnp.full(one.shape, EMPTY, F32)
    for one in totals:
        one[...] = jnp.ones(one.shape, F32)


def store_row_sums(tops, totals, sums_ref):
    def cell(s, carry):
        top = jnp.max(jnp.maximum(tops[0][s], tops[1][s]), axis=1, keepdims=True)
        total = totals[0][s] * jnp.exp2(tops[0][s] - top) + totals[1][s] * jnp.exp2(tops[1][s] - top)
        total = jnp.sum(total, axis=1, keepdims=True)
        sums_ref[pl.ds(s, 1), :] = to_lanes(top + jnp.log2(total))
        return carry

    lax.fori_loop(0, SRC_CELLS, cell, 0, unroll=4)


def table_copy(kept, ring, sem, step, out=False):
    slot = lax.rem(step, RING)
    ends = (ring.at[slot], kept.at[step])
    return pltpu.make_async_copy(*(ends if out else ends[::-1]), sem.at[slot])


def stream_start(kept, ring, sem, steps):
    for step in range(RING - 1):

        @pl.when(step < steps)
        def _():
            table_copy(kept, ring, sem, step).start()


def stream_step(kept, ring, sem, step, steps):
    table_copy(kept, ring, sem, step).wait()
    ahead = step + RING - 1

    @pl.when(ahead < steps)
    def _():
        table_copy(kept, ring, sem, ahead).start()

    return ring.at[lax.rem(step, RING)]


def first_kernel(places_s, places_t, scale, lists, s_order, t_order, arrived, *refs):
    ns, nt = len(places_s), len(places_t)
    s_refs, t_refs = refs[:ns], refs[ns : ns + nt]
    kept, sums_ref, first_ref, live_ref = refs[ns + nt : ns + nt + 4]
    xs, ys, level_ref, top0, top1, total0, total1, ring, s_sem, t_sem, sem = refs[ns + nt + 4 :]
    tops, totals = (top0, top1), (total0, total1)
    copies = load_targets(t_refs, places_t, t_order, ys, t_sem)
    copies += load_sources(s_refs, places_s, s_order, xs, s_sem)
    for copy in copies:
        copy.start()
    steps = lists[0]
    clear_stats(tops, totals)
    level_ref[LEVELS:, :] = jnp.full((8, PART), DEAD, F32)
    for place in range(TGT_CELLS):
        t = place // SIDE * SIDE + t_order[place % SIDE]
        for k in range(TILES):
            row = place * TILES + k
            level_ref[pl.ds(t * TILES + k, 1), :] = arrived[row : row + 1, :]
    first_ref[...] = level_ref[:LEVELS, :]
    for copy in copies:
        copy.wait()

    def source_cell(s, carry):
        mark = xs[part_of(s), :PART].astype(F32)
        dead = jnp.where(eye() & (mark > 0.5 * MARK), DEAD, 0.0)
        live_ref[pl.ds(s, 1), :] = jnp.sum(dead, axis=0, keepdims=True)
        return carry

    lax.fori_loop(0, SRC_CELLS, source_cell, 0, unroll=4)

    def step(i, carry):
        @pl.when(i >= RING)
        def _():
            table_copy(kept, ring, sem, i - RING, out=True).wait()

        slot = lax.rem(i, RING)
        for half in range(2):
            s, t = pair(lists, i, half)
            inner = lax.dot_general(
                xs[part_of(s), :], ys[cell_rows(t), :], (((1,), (1,)), ((), ())), preferred_element_type=F32
            )
            inner = inner * scale
            ring[slot, half] = inner
            scores = [inner[:, tile(k)] + level for k, level in enumerate(level_rows(level_ref, t))]
            row_stats(scores, s, tops[half], totals[half])
        table_copy(kept, ring, sem, i, out=True).start()
        return carry

    lax.fori_loop(0, steps, step, 0)
    store_row_sums(tops, totals, sums_ref)

    def settle(i, carry):
        table_copy(kept, ring, sem, i, out=True).wait()
        return carry

    lax.fori_loop(jnp.maximum(steps - RING, 0), steps, settle, 0)


def source_levels(parts, live):
    return jnp.where(live < 0.5 * DEAD, DEAD, -join([part[...] for part in parts]))


def spread_rows(level_ref, wide_ref):
    def cell(s, carry):
        wide_ref[s] = to_rows(level_ref[pl.ds(s, 1), :])
        return carry

    lax.fori_loop(0, SRC_CELLS, cell, 0, unroll=4)


def column_kernel(
    lists, r0, r1, r2, r3, live_ref, kept, sums_ref, level_ref, top0, top1, total0, total1, wide_ref, ring, sem
):
    tops, totals = (top0, top1), (total0, total1)
    steps = lists[0]
    stream_start(kept, ring, sem, steps)
    level_ref[...] = source_levels((r0, r1, r2, r3), live_ref[...])
    spread_rows(level_ref, wide_ref)
    clear_stats(tops, totals)

    def step(i, carry):
        table = stream_step(kept, ring, sem, i, steps)
        for half in range(2):
            s, t = pair(lists, i, half)
            level = wide_ref[s]
            old_tops, old_totals = tops[half][t], totals[half][t]
            for k in range(TILES):
                scores = (table[half, :, tile(k)] + level).reshape(PART // 8, 8, PART)
                top = jnp.maximum(old_tops[k], jnp.max(scores, axis=0))
                total = jnp.sum(jnp.exp2(scores - top[None]), axis=0)
                tops[half][t, k] = top
                totals[half][t, k] = old_totals[k] * jnp.exp2(old_tops[k] - top) + total
        return carry

    lax.fori_loop(0, steps, step, 0)
    tops = [one[:TGT_CELLS].reshape(LEVELS, 8, PART) for one in tops]
    totals = [one[:TGT_CELLS].reshape(LEVELS, 8, PART) for one in totals]
    top = jnp.max(jnp.maximum(*tops), axis=1)
    total = sum(part * jnp.exp2(one - top[:, None, :]) for one, part in zip(tops, totals))
    sums_ref[...] = top + jnp.log2(jnp.sum(total, axis=1))


def target_levels(joined, before, after, first_level, level_ref):
    own = -join([joined[: LEVELS // 2, :], before[...]])
    following = -join([joined[LEVELS // 2 :, :], after[...]])
    levels = jnp.concatenate([own, following], axis=0)
    level_ref[:LEVELS, :] = jnp.where(first_level[...] < 0.5 * DEAD, DEAD, levels)
    level_ref[LEVELS:, :] = jnp.full((8, PART), DEAD, F32)


def row_kernel(
    lists, joined, before, after, first_level, kept, sums_ref, level_ref, top0, top1, total0, total1, ring, sem
):
    tops, totals = (top0, top1), (total0, total1)
    steps = lists[0]
    stream_start(kept, ring, sem, steps)
    target_levels(joined, before, after, first_level, level_ref)
    clear_stats(tops, totals)

    def step(i, carry):
        table = stream_step(kept, ring, sem, i, steps)
        for half in range(2):
            s, t = pair(lists, i, half)
            scores = [table[half, :, tile(k)] + level for k, level in enumerate(level_rows(level_ref, t))]
            row_stats(scores, s, tops[half], totals[half])
        return carry

    lax.fori_loop(0, steps, step, 0)
    store_row_sums(tops, totals, sums_ref)


def pieces(value, count):
    found = []
    for _ in range(count):
        piece = value.astype(BF16).astype(F32)
        found.append(piece)
        value = value - piece
    return found


def transport_kernel(
    places_t, lists, t_order, joined, before, after, first_level, src_level, kept, *refs
):
    nt = len(places_t)
    t_refs = refs[:nt]
    out_ref, own_ref, ys, level_ref, wide_ref, map_ref, mass_ref, ring, t_sem, sem = refs[nt:]
    steps = lists[0]
    copies = load_targets(t_refs, places_t, t_order, ys, t_sem)
    for copy in copies:
        copy.start()
    stream_start(kept, ring, sem, steps)
    target_levels(joined, before, after, first_level, level_ref)
    spread_rows(src_level, wide_ref)
    for one in (map_ref, mass_ref):
        one[...] = jnp.zeros(one.shape, F32)
    for k, level in enumerate(level_rows(level_ref, t_order[0])):
        own_ref[k : k + 1, :] = level
    for copy in copies:
        copy.wait()

    def step(i, carry):
        table = stream_step(kept, ring, sem, i, steps)
        parts = []
        for half in range(2):
            s, t = pair(lists, i, half)
            level = wide_ref[s]
            weights = [
                jnp.exp2(table[half, :, tile(k)] + one + level).astype(BF16)
                for k, one in enumerate(level_rows(level_ref, t))
            ]
            part = jnp.dot(jnp.concatenate(weights, axis=1), ys[cell_rows(t), :], preferred_element_type=F32)
            parts.append((s, part, functools.reduce(jnp.add, [one.astype(F32) for one in weights])))
        for s, part, mass in parts:
            map_ref[s] += part
            mass_ref[s] += mass
        return carry

    lax.fori_loop(0, steps, step, 0)
    rows = lax.broadcasted_iota(jnp.int32, (TAIL, WIDTH), 0)

    def cell(s, carry):
        mass = to_lanes(jnp.sum(mass_ref[s], axis=1, keepdims=True))
        out_ref[s, :PART, :] = map_ref[s].astype(BF16)
        parts = pieces(mass, 2) + pieces(src_level[pl.ds(s, 1), :], 3)
        last = jnp.concatenate([parts[4]] * SIDE, axis=1)
        tail = jnp.where(rows == 0, jnp.concatenate(parts[:4], axis=1), jnp.where(rows == 1, last, 0.0))
        out_ref[s, PART:, :] = tail.astype(BF16)
        return carry

    lax.fori_loop(0, SRC_CELLS, cell, 0, unroll=2)


def finish_kernel(counts, got, own_level, half_src, half_tgt, src_ref, tgt_ref, map_ref):
    def tail(sender):
        return got[sender, PART:, :].astype(F32)

    def segment(rows, index):
        return rows[index // SIDE : index // SIDE + 1, index % SIDE * PART : (index % SIDE + 1) * PART]

    lanes = lax.broadcasted_iota(jnp.int32, (1, PART), 1)
    rows = lax.broadcasted_iota(jnp.int32, (PART, 1), 0)
    src_live, tgt_live = counts[0, 0], counts[0, 1]
    for q in range(SIDE):
        tails = [tail(q * SIDE + x) for x in range(SIDE)]
        weight_sum = sum(segment(one, 0) + segment(one, 1) for one in tails)
        live = rows + q * PART < src_live
        inverse = jnp.where(live, 1.0 / to_rows(weight_sum), 0.0)
        for chunk in range(WIDTH // PART):
            columns = slice(chunk * PART, (chunk + 1) * PART)
            numerator = sum(got[q * SIDE + x, :PART, columns].astype(F32) for x in range(SIDE))
            map_ref[q * PART : (q + 1) * PART, columns] = jnp.where(live, numerator * inverse, 0.0)
        level = segment(tails[0], 2) + segment(tails[0], 3) + segment(tails[0], 4)
        value = (level + half_src[q : q + 1, :]) * (EPSILON / LOG2E)
        src_ref[q : q + 1, :] = jnp.where(lanes + q * PART < src_live, value, 0.0)
        value = (own_level[q : q + 1, :] + half_tgt[q : q + 1, :]) * (EPSILON / LOG2E)
        tgt_ref[q : q + 1, :] = jnp.where(lanes + q * PART < tgt_live, value, 0.0)


VM = pl.BlockSpec(memory_space=pltpu.VMEM)
SM = pl.BlockSpec(memory_space=pltpu.SMEM)
ANY = pl.BlockSpec(memory_space=pl.ANY)


def call(kernel, out_shape, in_specs, scratch, *args, out_specs=None):
    outs = jax.tree.map(lambda _: VM, out_shape) if out_specs is None else out_specs
    return pl.pallas_call(
        kernel,
        out_shape=out_shape,
        in_specs=in_specs,
        out_specs=outs,
        scratch_shapes=scratch,
        compiler_params=pltpu.CompilerParams(vmem_limit_bytes=VMEM_LIMIT),
    )(*args)


def shape(*dims, dtype=F32):
    return jax.ShapeDtypeStruct(dims, dtype)


def half_norms(points, scale):
    return (0.5 * scale) * jnp.sum(jnp.square(points.astype(F32)), axis=1)


def shards(tiles, cell_slot, counts, src_points, tgt_points):
    help_index = lax.axis_index("help")
    src_index = lax.axis_index("src")
    z, x = help_index // SIDE, help_index % SIDE
    scale = LOG2E / (math.sqrt(WIDTH) * EPSILON)

    quarter = shape(PART, WIDTH, dtype=BF16)
    *quarters, marked_tgt = call(
        mark_kernel,
        (quarter,) * SIDE + (shape(WIDTH, WIDTH, dtype=BF16),),
        [SM, SM, VM, VM],
        [],
        counts,
        z[None],
        src_points,
        tgt_points,
    )
    next_first = to_group(marked_tgt, -1)
    parts = spread(quarters, z_perm)
    src_block = jnp.concatenate(parts, axis=0)
    _, later_tgt = lax.optimization_barrier((parts[1], marked_tgt))
    own = collect(later_tgt, z_perm)
    _, tiles, cell_slot = lax.optimization_barrier((own[1][2], tiles, cell_slot))
    around = jnp.concatenate([own[1][2], own[2][2]], axis=0)
    opposite = jnp.concatenate([own[3][2], own[4][2]], axis=0)
    own = [((0,), marked_tgt), ((1, 3), around), ((2,), opposite)]
    following = [((SIDE,), next_first)] + [
        (tuple(SIDE + cell for cell in cells), to_group(array, -1)) for cells, array in own[1:]
    ]
    sources = collect(src_block, x_perm)
    targets_all = own + following
    places_s = tuple((start, rows) for start, rows, _ in sources)
    places_t = tuple(cells for cells, _ in targets_all)
    s_arrays = [array for _, _, array in sources]
    t_arrays = [array for _, array in targets_all]
    halves = [half_norms(array, scale).reshape(-1, TILES, PART) for array in t_arrays]
    halves = [
        part for at in (0, 3) for part in (halves[at], halves[at + 1][:1], halves[at + 2], halves[at + 1][1:])
    ]
    halves = jnp.concatenate(halves).reshape(LEVELS, PART)
    arrived = jnp.where(halves > 1e7, DEAD, -halves)

    src_slot = lookup(tiles[0], cell_slot[0])
    tgt_slot = lookup(tiles[1], cell_slot[1])
    src_cell = src_slot % SRC_CELLS
    tgt_cell = tgt_slot % SRC_CELLS // SIDE + jnp.where(tgt_slot // SRC_CELLS == src_index, 0, SIDE)
    mine = tgt_slot % SIDE == x
    index = jnp.arange(PAIRS, dtype=jnp.int32)
    place = jnp.sum((mine[None, :] & (index[None, :] < index[:, None])).astype(jnp.int32), axis=1)
    hits = mine[None, :] & (place[None, :] == index[:, None])
    pair_src = jnp.sum(jnp.where(hits, src_cell[None, :], 0), axis=1)
    pair_tgt = jnp.sum(jnp.where(hits, tgt_cell[None, :] - NOBODY, 0), axis=1) + NOBODY
    steps = (jnp.sum(mine.astype(jnp.int32)) + 1) // 2
    lists = jnp.concatenate([steps[None], pair_src, pair_tgt])
    local = jnp.arange(SRC_CELLS, dtype=jnp.int32)
    s_order = (z - local % SIDE) % SIDE * SIDE + (x - local // SIDE) % SIDE
    t_order = (z - jnp.arange(SIDE, dtype=jnp.int32)) % SIDE

    sums, small = shape(SRC_CELLS, PART), shape(LEVELS, PART)
    levels = pltpu.VMEM((LEVELS + 8, PART), F32)
    wide = pltpu.VMEM((SRC_CELLS, PART, PART), F32)
    narrow = pltpu.VMEM((TGT_CELLS + 1, TILES, 8, PART), F32)
    ring = [pltpu.VMEM((RING, 2, PART, WIDTH), F32)]
    ring_sem = [pltpu.SemaphoreType.DMA((RING,))]
    t_sem = [pltpu.SemaphoreType.DMA((TGT_CELLS,))]
    kept, row_part, first_level, live = call(
        functools.partial(first_kernel, places_s, places_t, scale),
        (shape(STEPS, 2, PART, WIDTH), sums, small, sums),
        [SM] * 3 + [VM] + [ANY] * (len(s_arrays) + len(t_arrays)),
        [
            pltpu.VMEM((SRC_CELLS * PART, WIDTH), BF16),
            pltpu.VMEM((TGT_CELLS * WIDTH, WIDTH), BF16),
            levels,
        ]
        + [wide] * 4
        + ring
        + [pltpu.SemaphoreType.DMA((SRC_CELLS,))]
        + t_sem
        + ring_sem,
        lists,
        s_order,
        t_order,
        arrived,
        *s_arrays,
        *t_arrays,
        out_specs=(ANY, VM, VM, VM),
    )
    for sweep in range(ITERS):
        if sweep:
            row_part = call(
                row_kernel,
                sums,
                [SM] + [VM] * 4 + [ANY],
                [levels] + [wide] * 4 + ring + ring_sem,
                lists,
                joined,
                before,
                after,
                first_level,
                kept,
            )
        col_part, src_level = call(
            column_kernel,
            (small, sums),
            [SM] + [VM] * 5 + [ANY],
            [narrow] * 4 + [wide] + ring + ring_sem,
            lists,
            *ring_parts(row_part, x_perm),
            live,
            kept,
        )
        joined = join(ring_parts(col_part, z_perm))
        before = to_group(joined[LEVELS // 2 :], 1)
        after = to_group(joined[: LEVELS // 2], -1)
    blocks, own_level = call(
        functools.partial(transport_kernel, places_t),
        (shape(SRC_CELLS, PART + TAIL, WIDTH, dtype=BF16), shape(SIDE, PART)),
        [SM] * 2 + [VM] * 5 + [ANY] * (1 + len(t_arrays)),
        [pltpu.VMEM((TGT_CELLS * WIDTH, WIDTH), BF16), levels, wide]
        + [pltpu.VMEM((SRC_CELLS, PART, WIDTH), F32), wide]
        + ring
        + t_sem
        + ring_sem,
        lists,
        t_order,
        joined,
        before,
        after,
        first_level,
        src_level,
        kept,
        *t_arrays,
    )
    got = lax.all_to_all(blocks, "help", 0, 0)
    _, src_after, tgt_after = lax.optimization_barrier((src_level, src_points, tgt_points))
    half_src = half_norms(src_after, scale).reshape(SIDE, PART)
    half_tgt = half_norms(tgt_after, scale).reshape(SIDE, PART)
    source_out, target_out, transport = call(
        finish_kernel,
        (shape(SIDE, PART), shape(SIDE, PART), shape(SIDE * PART, WIDTH)),
        [SM] + [VM] * 4,
        [],
        counts,
        got,
        own_level,
        half_src,
        half_tgt,
    )
    return (source_out.reshape(-1), target_out.reshape(-1), transport)


def solution(mesh):
    in_specs = (
        P(None, "src"),
        P(),
        P(("src", "help"), None),
        P(("src", "help"), None),
        P(("src", "help"), None),
    )
    out_specs = (P(("src", "help")), P(("src", "help")), P(("src", "help"), None))
    return jax.shard_map(shards, mesh=mesh, in_specs=in_specs, out_specs=out_specs, check_vma=False)
```

```python
import functools
import math

import jax
import jax.numpy as jnp
from jax import lax
from jax.experimental import pallas as pl
from jax.experimental.pallas import tpu as pltpu
from jax.sharding import PartitionSpec as P

ITERS = 2
EPSILON = 0.2
LOG2E = 1.0 / math.log(2.0)
DEAD = -1e30
EMPTY = -2e30
MARK = 1024.0
SIDE = 4
PART = 128
WIDTH = 512
SRC_CELLS = 16
TGT_CELLS = 8
TILES = WIDTH // PART
LEVELS = TGT_CELLS * TILES
TAIL = 16
PAIRS = 128
STEPS = PAIRS // 2
RING = 12
NOBODY = TGT_CELLS
F32 = jnp.float32
BF16 = jnp.bfloat16
VMEM_LIMIT = 28 * 1024 * 1024


def x_perm(by):
    return [(z * SIDE + x, z * SIDE + (x + by) % SIDE) for z in range(SIDE) for x in range(SIDE)]


def z_perm(by):
    return [(z * SIDE + x, (z + by) % SIDE * SIDE + x) for z in range(SIDE) for x in range(SIDE)]


def to_group(array, by):
    count = lax.axis_size("src")
    return lax.ppermute(array, "src", [(i, (i + by) % count) for i in range(count)])


def to_help(array, perm):
    return lax.ppermute(array, "help", perm)


def lookup(cell_ids, slot_table):
    matches = cell_ids[:, None] == jnp.arange(slot_table.shape[0], dtype=jnp.int32)[None, :]
    return jnp.sum(jnp.where(matches, slot_table[None, :], 0), axis=1)


def mark_kernel(counts, place, src_ref, tgt_ref, q0, q1, q2, q3, marked_ref):
    rows = lax.broadcasted_iota(jnp.int32, (PART, WIDTH), 0)

    def marked(ref, q, count, mark):
        points = ref[part_of(q), :].astype(F32)
        return jnp.where(rows + q * PART < count, points, mark).astype(BF16)

    for by, out in enumerate((q0, q1, q2, q3)):
        out[...] = marked(src_ref, lax.rem(place[0] + by, SIDE), counts[0, 0], MARK)
    for q in range(SIDE):
        marked_ref[q * PART : (q + 1) * PART, :] = marked(tgt_ref, q, counts[0, 1], -MARK)


def spread(parts, perm):
    return [part if by == 0 else to_help(part, perm(by)) for by, part in enumerate(parts)]


def collect(block, perm):
    rows = block.shape[0]
    half = rows // 2
    behind = to_help(block, perm(1))
    ahead = to_help(block, perm(SIDE - 1))
    far_low = to_help(behind[:half], perm(1))
    far_high = to_help(ahead[half:], perm(SIDE - 1))
    return [
        (0, rows, block),
        (rows, rows, behind),
        (3 * rows, rows, ahead),
        (2 * rows, half, far_low),
        (2 * rows + half, half, far_high),
    ]


def ring_parts(array, perm):
    return [array] + [to_help(array, perm(by)) for by in range(1, SIDE)]


def join(parts):
    top = functools.reduce(jnp.maximum, parts)
    total = functools.reduce(jnp.add, [jnp.exp2(part - top) for part in parts])
    return top + jnp.log2(total)


def eye():
    return lax.broadcasted_iota(jnp.int32, (PART, PART), 0) == lax.broadcasted_iota(
        jnp.int32, (PART, PART), 1
    )


def to_lanes(column):
    return jnp.sum(jnp.where(eye(), jnp.broadcast_to(column, (PART, PART)), 0.0), axis=0, keepdims=True)


def to_rows(lane_vector):
    return jnp.transpose(jnp.broadcast_to(lane_vector, (PART, PART)))


def part_of(index):
    return pl.ds(pl.multiple_of(index * PART, PART), PART)


def load_sources(refs, places, order, target, sem):
    copies = []
    for (start, rows), ref in zip(places, refs):
        for cell in range(rows // PART):
            copies.append(
                pltpu.make_async_copy(
                    ref.at[pl.ds(cell * PART, PART)],
                    target.at[part_of(order[start // PART + cell])],
                    sem.at[len(copies)],
                )
            )
    return copies


def load_targets(refs, places, order, target, sem):
    copies = []
    for cells, ref in zip(places, refs):
        for index, cell in enumerate(cells):
            side, place = cell // SIDE, cell % SIDE
            copies.append(
                pltpu.make_async_copy(
                    ref.at[pl.ds(index * WIDTH, WIDTH)],
                    target.at[cell_rows(side * SIDE + order[place])],
                    sem.at[len(copies)],
                )
            )
    return copies


def tile(k):
    return slice(k * PART, (k + 1) * PART)


def cell_rows(t):
    return pl.ds(pl.multiple_of(lax.rem(t, NOBODY) * WIDTH, WIDTH), WIDTH)


def pair(lists, i, half):
    place = 2 * i + half
    return lists[1 + place], lists[1 + PAIRS + place]


def level_rows(level_ref, t):
    return [level_ref[pl.ds(t * TILES + k, 1), :] for k in range(TILES)]


def row_stats(scores, s, tops, totals):
    old = tops[s]
    top = functools.reduce(jnp.maximum, scores, old)
    total = functools.reduce(jnp.add, [jnp.exp2(one - top) for one in scores])
    totals[s] = totals[s] * jnp.exp2(old - top) + total
    tops[s] = top


def clear_stats(tops, totals):
    for one in tops:
        one[...] = jnp.full(one.shape, EMPTY, F32)
    for one in totals:
        one[...] = jnp.ones(one.shape, F32)


def store_row_sums(tops, totals, sums_ref):
    def cell(s, carry):
        top = jnp.max(jnp.maximum(tops[0][s], tops[1][s]), axis=1, keepdims=True)
        total = totals[0][s] * jnp.exp2(tops[0][s] - top) + totals[1][s] * jnp.exp2(tops[1][s] - top)
        total = jnp.sum(total, axis=1, keepdims=True)
        sums_ref[pl.ds(s, 1), :] = to_lanes(top + jnp.log2(total))
        return carry

    lax.fori_loop(0, SRC_CELLS, cell, 0, unroll=8)


def table_copy(kept, ring, sem, step, out=False):
    slot = lax.rem(step, RING)
    ends = (ring.at[slot], kept.at[step])
    return pltpu.make_async_copy(*(ends if out else ends[::-1]), sem.at[slot])


def stream_start(kept, ring, sem, steps):
    for step in range(RING - 1):

        @pl.when(step < steps)
        def _():
            table_copy(kept, ring, sem, step).start()


def stream_step(kept, ring, sem, step, steps):
    table_copy(kept, ring, sem, step).wait()
    ahead = step + RING - 1

    @pl.when(ahead < steps)
    def _():
        table_copy(kept, ring, sem, ahead).start()

    return ring.at[lax.rem(step, RING)]


def first_kernel(places_s, places_t, scale, lists, s_order, t_order, arrived, *refs):
    ns, nt = len(places_s), len(places_t)
    s_refs, t_refs = refs[:ns], refs[ns : ns + nt]
    kept, sums_ref, first_ref, live_ref = refs[ns + nt : ns + nt + 4]
    xs, ys, level_ref, top0, top1, total0, total1, ring, s_sem, t_sem, sem = refs[ns + nt + 4 :]
    tops, totals = (top0, top1), (total0, total1)
    copies = load_targets(t_refs, places_t, t_order, ys, t_sem)
    copies += load_sources(s_refs, places_s, s_order, xs, s_sem)
    for copy in copies:
        copy.start()
    steps = lists[0]
    clear_stats(tops, totals)
    level_ref[LEVELS:, :] = jnp.full((8, PART), DEAD, F32)
    for place in range(TGT_CELLS):
        t = place // SIDE * SIDE + t_order[place % SIDE]
        for k in range(TILES):
            row = place * TILES + k
            level_ref[pl.ds(t * TILES + k, 1), :] = arrived[row : row + 1, :]
    first_ref[...] = level_ref[:LEVELS, :]
    for copy in copies:
        copy.wait()

    def source_cell(s, carry):
        mark = xs[part_of(s), :PART].astype(F32)
        dead = jnp.where(eye() & (mark > 0.5 * MARK), DEAD, 0.0)
        live_ref[pl.ds(s, 1), :] = jnp.sum(dead, axis=0, keepdims=True)
        return carry

    lax.fori_loop(0, SRC_CELLS, source_cell, 0, unroll=8)

    def step(i, carry):
        @pl.when(i >= RING)
        def _():
            table_copy(kept, ring, sem, i - RING, out=True).wait()

        slot = lax.rem(i, RING)
        for half in range(2):
            s, t = pair(lists, i, half)
            inner = lax.dot_general(
                xs[part_of(s), :], ys[cell_rows(t), :], (((1,), (1,)), ((), ())), preferred_element_type=F32
            )
            inner = inner * scale
            ring[slot, half] = inner
            scores = [inner[:, tile(k)] + level for k, level in enumerate(level_rows(level_ref, t))]
            row_stats(scores, s, tops[half], totals[half])
        table_copy(kept, ring, sem, i, out=True).start()
        return carry

    lax.fori_loop(0, steps, step, 0)
    store_row_sums(tops, totals, sums_ref)

    def settle(i, carry):
        table_copy(kept, ring, sem, i, out=True).wait()
        return carry

    lax.fori_loop(jnp.maximum(steps - RING, 0), steps, settle, 0)


def source_levels(parts, live):
    return jnp.where(live < 0.5 * DEAD, DEAD, -join([part[...] for part in parts]))


def spread_rows(level_ref, wide_ref):
    def cell(s, carry):
        wide_ref[s] = to_rows(level_ref[pl.ds(s, 1), :])
        return carry

    lax.fori_loop(0, SRC_CELLS, cell, 0, unroll=8)


def column_kernel(
    lists, r0, r1, r2, r3, live_ref, kept, sums_ref, level_ref, top0, top1, total0, total1, wide_ref, ring, sem
):
    tops, totals = (top0, top1), (total0, total1)
    steps = lists[0]
    stream_start(kept, ring, sem, steps)
    level_ref[...] = source_levels((r0, r1, r2, r3), live_ref[...])
    spread_rows(level_ref, wide_ref)
    clear_stats(tops, totals)

    def step(i, carry):
        table = stream_step(kept, ring, sem, i, steps)
        for half in range(2):
            s, t = pair(lists, i, half)
            level = wide_ref[s]
            old_tops, old_totals = tops[half][t], totals[half][t]
            for k in range(TILES):
                scores = (table[half, :, tile(k)] + level).reshape(PART // 8, 8, PART)
                top = jnp.maximum(old_tops[k], jnp.max(scores, axis=0))
                total = jnp.sum(jnp.exp2(scores - top[None]), axis=0)
                tops[half][t, k] = top
                totals[half][t, k] = old_totals[k] * jnp.exp2(old_tops[k] - top) + total
        return carry

    lax.fori_loop(0, steps, step, 0)
    tops = [one[:TGT_CELLS].reshape(LEVELS, 8, PART) for one in tops]
    totals = [one[:TGT_CELLS].reshape(LEVELS, 8, PART) for one in totals]
    top = jnp.max(jnp.maximum(*tops), axis=1)
    total = sum(part * jnp.exp2(one - top[:, None, :]) for one, part in zip(tops, totals))
    sums_ref[...] = top + jnp.log2(jnp.sum(total, axis=1))


def target_levels(joined, before, after, first_level, level_ref):
    own = -join([joined[: LEVELS // 2, :], before[...]])
    following = -join([joined[LEVELS // 2 :, :], after[...]])
    levels = jnp.concatenate([own, following], axis=0)
    level_ref[:LEVELS, :] = jnp.where(first_level[...] < 0.5 * DEAD, DEAD, levels)
    level_ref[LEVELS:, :] = jnp.full((8, PART), DEAD, F32)


def row_kernel(
    lists, joined, before, after, first_level, kept, sums_ref, level_ref, top0, top1, total0, total1, ring, sem
):
    tops, totals = (top0, top1), (total0, total1)
    steps = lists[0]
    stream_start(kept, ring, sem, steps)
    target_levels(joined, before, after, first_level, level_ref)
    clear_stats(tops, totals)

    def step(i, carry):
        table = stream_step(kept, ring, sem, i, steps)
        for half in range(2):
            s, t = pair(lists, i, half)
            scores = [table[half, :, tile(k)] + level for k, level in enumerate(level_rows(level_ref, t))]
            row_stats(scores, s, tops[half], totals[half])
        return carry

    lax.fori_loop(0, steps, step, 0)
    store_row_sums(tops, totals, sums_ref)


def pieces(value, count):
    found = []
    for _ in range(count):
        piece = value.astype(BF16).astype(F32)
        found.append(piece)
        value = value - piece
    return found


def transport_kernel(
    places_t, lists, t_order, joined, before, after, first_level, src_level, kept, *refs
):
    nt = len(places_t)
    t_refs = refs[:nt]
    out_ref, own_ref, ys, level_ref, wide_ref, map_ref, mass_ref, ring, t_sem, sem = refs[nt:]
    steps = lists[0]
    copies = load_targets(t_refs, places_t, t_order, ys, t_sem)
    for copy in copies:
        copy.start()
    stream_start(kept, ring, sem, steps)
    target_levels(joined, before, after, first_level, level_ref)
    spread_rows(src_level, wide_ref)
    for one in (map_ref, mass_ref):
        one[...] = jnp.zeros(one.shape, F32)
    for k, level in enumerate(level_rows(level_ref, t_order[0])):
        own_ref[k : k + 1, :] = level
    for copy in copies:
        copy.wait()

    def step(i, carry):
        table = stream_step(kept, ring, sem, i, steps)
        parts = []
        for half in range(2):
            s, t = pair(lists, i, half)
            level = wide_ref[s]
            weights = [
                jnp.exp2(table[half, :, tile(k)] + one + level).astype(BF16)
                for k, one in enumerate(level_rows(level_ref, t))
            ]
            part = jnp.dot(jnp.concatenate(weights, axis=1), ys[cell_rows(t), :], preferred_element_type=F32)
            parts.append((s, part, functools.reduce(jnp.add, [one.astype(F32) for one in weights])))
        for s, part, mass in parts:
            map_ref[s] += part
            mass_ref[s] += mass
        return carry

    lax.fori_loop(0, steps, step, 0)
    rows = lax.broadcasted_iota(jnp.int32, (TAIL, WIDTH), 0)

    def cell(s, carry):
        mass = to_lanes(jnp.sum(mass_ref[s], axis=1, keepdims=True))
        out_ref[s, :PART, :] = map_ref[s].astype(BF16)
        parts = pieces(mass, 2) + pieces(src_level[pl.ds(s, 1), :], 3)
        last = jnp.concatenate([parts[4]] * SIDE, axis=1)
        tail = jnp.where(rows == 0, jnp.concatenate(parts[:4], axis=1), jnp.where(rows == 1, last, 0.0))
        out_ref[s, PART:, :] = tail.astype(BF16)
        return carry

    lax.fori_loop(0, SRC_CELLS, cell, 0, unroll=2)


def finish_kernel(counts, got, own_level, half_src, half_tgt, src_ref, tgt_ref, map_ref):
    def tail(sender):
        return got[sender, PART:, :].astype(F32)

    def segment(rows, index):
        return rows[index // SIDE : index // SIDE + 1, index % SIDE * PART : (index % SIDE + 1) * PART]

    lanes = lax.broadcasted_iota(jnp.int32, (1, PART), 1)
    rows = lax.broadcasted_iota(jnp.int32, (PART, 1), 0)
    src_live, tgt_live = counts[0, 0], counts[0, 1]
    for q in range(SIDE):
        tails = [tail(q * SIDE + x) for x in range(SIDE)]
        weight_sum = sum(segment(one, 0) + segment(one, 1) for one in tails)
        live = rows + q * PART < src_live
        inverse = jnp.where(live, 1.0 / to_rows(weight_sum), 0.0)
        for chunk in range(WIDTH // PART):
            columns = slice(chunk * PART, (chunk + 1) * PART)
            numerator = sum(got[q * SIDE + x, :PART, columns].astype(F32) for x in range(SIDE))
            map_ref[q * PART : (q + 1) * PART, columns] = jnp.where(live, numerator * inverse, 0.0)
        level = segment(tails[0], 2) + segment(tails[0], 3) + segment(tails[0], 4)
        value = (level + half_src[q : q + 1, :]) * (EPSILON / LOG2E)
        src_ref[q : q + 1, :] = jnp.where(lanes + q * PART < src_live, value, 0.0)
        value = (own_level[q : q + 1, :] + half_tgt[q : q + 1, :]) * (EPSILON / LOG2E)
        tgt_ref[q : q + 1, :] = jnp.where(lanes + q * PART < tgt_live, value, 0.0)


VM = pl.BlockSpec(memory_space=pltpu.VMEM)
SM = pl.BlockSpec(memory_space=pltpu.SMEM)
ANY = pl.BlockSpec(memory_space=pl.ANY)


def call(kernel, out_shape, in_specs, scratch, *args, out_specs=None):
    outs = jax.tree.map(lambda _: VM, out_shape) if out_specs is None else out_specs
    return pl.pallas_call(
        kernel,
        out_shape=out_shape,
        in_specs=in_specs,
        out_specs=outs,
        scratch_shapes=scratch,
        compiler_params=pltpu.CompilerParams(vmem_limit_bytes=VMEM_LIMIT),
    )(*args)


def shape(*dims, dtype=F32):
    return jax.ShapeDtypeStruct(dims, dtype)


def half_norms(points, scale):
    return (0.5 * scale) * jnp.sum(jnp.square(points.astype(F32)), axis=1)


def shards(tiles, cell_slot, counts, src_points, tgt_points):
    help_index = lax.axis_index("help")
    src_index = lax.axis_index("src")
    z, x = help_index // SIDE, help_index % SIDE
    scale = LOG2E / (math.sqrt(WIDTH) * EPSILON)

    quarter = shape(PART, WIDTH, dtype=BF16)
    *quarters, marked_tgt = call(
        mark_kernel,
        (quarter,) * SIDE + (shape(WIDTH, WIDTH, dtype=BF16),),
        [SM, SM, VM, VM],
        [],
        counts,
        z[None],
        src_points,
        tgt_points,
    )
    next_first = to_group(marked_tgt, -1)
    parts = spread(quarters, z_perm)
    src_block = jnp.concatenate(parts, axis=0)
    _, later_tgt = lax.optimization_barrier((parts[1], marked_tgt))
    own = collect(later_tgt, z_perm)
    _, tiles, cell_slot = lax.optimization_barrier((own[1][2], tiles, cell_slot))
    around = jnp.concatenate([own[1][2], own[2][2]], axis=0)
    opposite = jnp.concatenate([own[3][2], own[4][2]], axis=0)
    own = [((0,), marked_tgt), ((1, 3), around), ((2,), opposite)]
    following = [((SIDE,), next_first)] + [
        (tuple(SIDE + cell for cell in cells), to_group(array, -1)) for cells, array in own[1:]
    ]
    sources = collect(src_block, x_perm)
    targets_all = own + following
    places_s = tuple((start, rows) for start, rows, _ in sources)
    places_t = tuple(cells for cells, _ in targets_all)
    s_arrays = [array for _, _, array in sources]
    t_arrays = [array for _, array in targets_all]
    halves = [half_norms(array, scale).reshape(-1, TILES, PART) for array in t_arrays]
    halves = [
        part for at in (0, 3) for part in (halves[at], halves[at + 1][:1], halves[at + 2], halves[at + 1][1:])
    ]
    halves = jnp.concatenate(halves).reshape(LEVELS, PART)
    arrived = jnp.where(halves > 1e7, DEAD, -halves)

    src_slot = lookup(tiles[0], cell_slot[0])
    tgt_slot = lookup(tiles[1], cell_slot[1])
    src_cell = src_slot % SRC_CELLS
    tgt_cell = tgt_slot % SRC_CELLS // SIDE + jnp.where(tgt_slot // SRC_CELLS == src_index, 0, SIDE)
    mine = tgt_slot % SIDE == x
    index = jnp.arange(PAIRS, dtype=jnp.int32)
    place = jnp.sum((mine[None, :] & (index[None, :] < index[:, None])).astype(jnp.int32), axis=1)
    hits = mine[None, :] & (place[None, :] == index[:, None])
    pair_src = jnp.sum(jnp.where(hits, src_cell[None, :], 0), axis=1)
    pair_tgt = jnp.sum(jnp.where(hits, tgt_cell[None, :] - NOBODY, 0), axis=1) + NOBODY
    steps = (jnp.sum(mine.astype(jnp.int32)) + 1) // 2
    lists = jnp.concatenate([steps[None], pair_src, pair_tgt])
    local = jnp.arange(SRC_CELLS, dtype=jnp.int32)
    s_order = (z - local % SIDE) % SIDE * SIDE + (x - local // SIDE) % SIDE
    t_order = (z - jnp.arange(SIDE, dtype=jnp.int32)) % SIDE

    sums, small = shape(SRC_CELLS, PART), shape(LEVELS, PART)
    levels = pltpu.VMEM((LEVELS + 8, PART), F32)
    wide = pltpu.VMEM((SRC_CELLS, PART, PART), F32)
    narrow = pltpu.VMEM((TGT_CELLS + 1, TILES, 8, PART), F32)
    ring = [pltpu.VMEM((RING, 2, PART, WIDTH), F32)]
    ring_sem = [pltpu.SemaphoreType.DMA((RING,))]
    t_sem = [pltpu.SemaphoreType.DMA((TGT_CELLS,))]
    kept, row_part, first_level, live = call(
        functools.partial(first_kernel, places_s, places_t, scale),
        (shape(STEPS, 2, PART, WIDTH), sums, small, sums),
        [SM] * 3 + [VM] + [ANY] * (len(s_arrays) + len(t_arrays)),
        [
            pltpu.VMEM((SRC_CELLS * PART, WIDTH), BF16),
            pltpu.VMEM((TGT_CELLS * WIDTH, WIDTH), BF16),
            levels,
        ]
        + [wide] * 4
        + ring
        + [pltpu.SemaphoreType.DMA((SRC_CELLS,))]
        + t_sem
        + ring_sem,
        lists,
        s_order,
        t_order,
        arrived,
        *s_arrays,
        *t_arrays,
        out_specs=(ANY, VM, VM, VM),
    )
    for sweep in range(ITERS):
        if sweep:
            row_part = call(
                row_kernel,
                sums,
                [SM] + [VM] * 4 + [ANY],
                [levels] + [wide] * 4 + ring + ring_sem,
                lists,
                joined,
                before,
                after,
                first_level,
                kept,
            )
        col_part, src_level = call(
            column_kernel,
            (small, sums),
            [SM] + [VM] * 5 + [ANY],
            [narrow] * 4 + [wide] + ring + ring_sem,
            lists,
            *ring_parts(row_part, x_perm),
            live,
            kept,
        )
        joined = join(ring_parts(col_part, z_perm))
        before = to_group(joined[LEVELS // 2 :], 1)
        after = to_group(joined[: LEVELS // 2], -1)
    blocks, own_level = call(
        functools.partial(transport_kernel, places_t),
        (shape(SRC_CELLS, PART + TAIL, WIDTH, dtype=BF16), shape(SIDE, PART)),
        [SM] * 2 + [VM] * 5 + [ANY] * (1 + len(t_arrays)),
        [pltpu.VMEM((TGT_CELLS * WIDTH, WIDTH), BF16), levels, wide]
        + [pltpu.VMEM((SRC_CELLS, PART, WIDTH), F32), wide]
        + ring
        + t_sem
        + ring_sem,
        lists,
        t_order,
        joined,
        before,
        after,
        first_level,
        src_level,
        kept,
        *t_arrays,
    )
    got = lax.all_to_all(blocks, "help", 0, 0)
    _, src_after, tgt_after = lax.optimization_barrier((src_level, src_points, tgt_points))
    half_src = half_norms(src_after, scale).reshape(SIDE, PART)
    half_tgt = half_norms(tgt_after, scale).reshape(SIDE, PART)
    source_out, target_out, transport = call(
        finish_kernel,
        (shape(SIDE, PART), shape(SIDE, PART), shape(SIDE * PART, WIDTH)),
        [SM] + [VM] * 4,
        [],
        counts,
        got,
        own_level,
        half_src,
        half_tgt,
    )
    return (source_out.reshape(-1), target_out.reshape(-1), transport)


def solution(mesh):
    in_specs = (
        P(None, "src"),
        P(),
        P(("src", "help"), None),
        P(("src", "help"), None),
        P(("src", "help"), None),
    )
    out_specs = (P(("src", "help")), P(("src", "help")), P(("src", "help"), None))
    return jax.shard_map(shards, mesh=mesh, in_specs=in_specs, out_specs=out_specs, check_vma=False)
```
